32 devices in a mesh: grp: 2 (over x), subj: 2 (over core), depth: 8 (over z, y).
Axes of the slice: x: 2, y: 2, z: 4, core: 2. Of those that a mesh axis runs over, the one named last changes fastest.
Arguments:
- template: bfloat16 [2, 4, 512, 4096], P('subj', None, 'depth'), may hold values from -6 to 6
- owner: int32 [4], replicated, may hold values from 0 to 1
- order: int32 [4, 4], P(('grp', 'subj')), parts along dimension 0, may hold values from 0 to 3, each once within a row
- subject: float32 [4, 4, 512, 4096], P(('grp', 'subj'), None, 'depth'), parts along dimension 0, may hold values from -6 to 6
- displacement: float32 [4, 3, 512, 4096], P(('grp', 'subj'), None, 'depth'), parts along dimension 0, may hold values from -3 to 3
Outputs:
- updated: float32 [4, 3, 512, 4096], P(('grp', 'subj'), None, 'depth'), parts along dimension 0
The draws below stay inside these ranges and needn't reach their ends.
There are 2 independent parts, one for each index of `grp`. The reference program is written for one: setup_inputs(seed, part) draws one part's arguments, and reference() takes and returns one part's arrays. A program takes and returns all parts, laid end to end along the dimension named above; an argument that names none is the same for every part. Nothing has to cross between parts.
Inputs may be any that keep to these rules, and one draw needn't show every extreme that they name: owner[k] is the slot of template that holds stain k. Every row of order holds each stain once.
All inputs are finite; a program needn't handle non-finite values.
Results may differ from the reference program's by a relative error of at most 0.0003.
Values may be sent and summed in bfloat16 or wider, within the bound.
No kernel may reach another device: no remote copies, remote signals or barrier semaphores. Data moves between devices by JAX's collectives and lax.ppermute only.
A program may use at most 128 MiB of HBM per device.

```python
import jax
import jax.numpy as jnp

GY = 64
STAINS = 4
SWEEPS = 4
SUBJECTS = 2
DEPTH = 512
SLOTS = 2
CELLS = 4096
N_SUBJ = 2


def place_ends(drawn, key, smallest, largest):
    shape = drawn.shape
    index_at = [jax.random.randint(jax.random.fold_in(key, axis), (), 0, shape[axis]) for axis in range(len(shape))]
    drawn = drawn.at[tuple(index_at)].set(smallest)
    longest = shape.index(max(shape))
    index_at[longest] = (index_at[longest] + 1) % shape[longest]
    return drawn.at[tuple(index_at)].set(largest)


def steps_of(own_key, dims, cuts, smallest, largest):
    level = 1.0
    for dim, parts in cuts:
        heights = jax.random.uniform(jax.random.fold_in(jax.random.fold_in(own_key, 6), dim), (parts,), jnp.float32, smallest / len(cuts), largest / len(cuts))
        level = level * jnp.repeat(jnp.exp(heights), dims[dim] // parts).reshape((-1,) + (1,) * (len(dims) - 1 - dim))
    return level


def centred(key, shape, scale, reach, shards=(), held_as=jnp.bfloat16):
    drawn = jax.random.normal(key, shape, jnp.float32) * scale
    if len(shards) > 0:
        drawn = steps_of(key, shape, shards, -0.22, 0.18) * drawn
    return jnp.clip(drawn, min=-reach, max=reach).astype(held_as)


def setup_inputs(seed: int = 0, part: int = 0) -> dict:
    streams_of = jax.random.split(jax.random.key(seed), 6)
    part_splits = jax.random.split(jax.random.fold_in(streams_of[5], part), 6)
    return {
        "template": centred(streams_of[0], (SLOTS, STAINS, DEPTH, CELLS), 1.0, 6.0, ((0, 2), (2, 8))),
        "owner": place_ends(jax.random.randint(streams_of[1], (STAINS,), 0, N_SUBJ), jax.random.fold_in(streams_of[1], 1), 0, N_SUBJ - 1).astype(jnp.int32),
        "order": jax.vmap(lambda own: jax.random.permutation(own, STAINS))(jax.random.split(part_splits[2], SUBJECTS)).reshape((SUBJECTS, STAINS)).astype(jnp.int32),
        "subject": centred(part_splits[3], (SUBJECTS, STAINS, DEPTH, CELLS), 1.0, 6.0, ((0, 2), (2, 8)), jnp.float32),
        "displacement": centred(part_splits[4], (SUBJECTS, 3, DEPTH, CELLS), 0.5, 3.0, ((0, 2), (2, 8)), jnp.float32),
    }


step_size = 1.0
smooth_rate = 0.15
force_floor = 0.5


def shift_cells(a, offset):
    zeros = jnp.zeros(a.shape[:-1] + (abs(offset),), a.dtype)
    if offset > 0:
        return jnp.concatenate([a[..., offset:], zeros], axis=-1)
    return jnp.concatenate([zeros, a[..., :offset]], axis=-1)


def lateral_parts(a):
    column = jnp.arange(a.shape[-1]) % GY
    x_plus = shift_cells(a, GY)
    x_minus = shift_cells(a, -GY)
    y_plus = jnp.where(column < GY - 1, shift_cells(a, 1), 0.0)
    y_minus = jnp.where(column > 0, shift_cells(a, -1), 0.0)
    return x_plus, x_minus, y_plus, y_minus


def gradients(padded):
    centre = padded[..., 1:-1, :]
    x_plus, x_minus, y_plus, y_minus = lateral_parts(centre)
    grad_x = (x_plus - x_minus) * 0.5
    grad_y = (y_plus - y_minus) * 0.5
    grad_z = (padded[..., 2:, :] - padded[..., :-2, :]) * 0.5
    return grad_x, grad_y, grad_z, centre


def sweep(padded):
    centre = padded[..., 1:-1, :]
    x_plus, x_minus, y_plus, y_minus = lateral_parts(centre)
    total = padded[..., 2:, :] + padded[..., :-2, :] + x_plus + x_minus + y_plus + y_minus
    return centre + smooth_rate * (total - 6.0 * centre)


def pad_depth(a, width):
    spec = [(0, 0)] * (a.ndim - 2) + [(width, width), (0, 0)]
    return jnp.pad(a, spec)


def reference(template, owner, order, subject, displacement):
    fixed = template[owner, jnp.arange(STAINS)].astype(jnp.float32)
    results = []
    for s in range(SUBJECTS):
        grad_x, grad_y, grad_z, centre = gradients(pad_depth(subject[s], 1))
        u = displacement[s]
        for j in range(STAINS):
            k = order[s, j]
            gx = grad_x[k]
            gy = grad_y[k]
            gz = grad_z[k]
            diff = fixed[k] - (centre[k] + gx * u[0] + gy * u[1] + gz * u[2])
            denom = gx * gx + gy * gy + gz * gz + diff * diff + force_floor
            u = u + step_size * diff[None] * jnp.stack([gx, gy, gz], 0) / denom[None]
        for i in range(SWEEPS):
            u = sweep(pad_depth(u, 1))
        results.append(u)
    return jnp.stack(results, 0)
```

```python
import functools

import jax
import jax.numpy as jnp
from jax import lax
from jax.experimental import pallas as pl
from jax.experimental.pallas import tpu as pltpu
from jax.sharding import PartitionSpec as P

GY = 64
SWEEPS = 4
LANES = 128
RATE = 0.15
F32 = jnp.float32
BF16 = jnp.bfloat16
EDGE = 16

ANY = pl.BlockSpec(memory_space=pl.ANY)
VMEM = pl.BlockSpec(memory_space=pltpu.VMEM)
SMEM = pl.BlockSpec(memory_space=pltpu.SMEM)


def params():
    return pltpu.CompilerParams(vmem_limit_bytes=48 << 20)


def pair_swaps(count):
    def swaps(first):
        return [p for i in range(first, count - 1, 2) for p in ((i, i + 1), (i + 1, i))]

    return swaps(0), swaps(1)


def lateral_matrix(difference):
    row = lax.broadcasted_iota(jnp.int32, (2 * LANES, 2 * LANES), 0) & (LANES - 1)
    col = lax.broadcasted_iota(jnp.int32, (2 * LANES, 2 * LANES), 1)
    right = col >= LANES
    col = col & (LANES - 1)
    swap = jnp.where((row ^ col) == GY, 1.0, 0.0)
    same = (row & GY) == (col & GY)
    plus = jnp.where((row == col + 1) & same, 1.0, 0.0)
    minus = jnp.where((row == col - 1) & same, 1.0, 0.0)
    left = plus - minus if difference else plus + minus + swap
    return jnp.where(right, swap, left).astype(BF16)


def lateral(x, matrix):
    high = x.astype(BF16)
    low = (x - high.astype(F32)).astype(BF16)
    return jnp.dot(jnp.concatenate([high, low], 1), matrix, preferred_element_type=F32)


def low_half(rows):
    return lax.broadcasted_iota(jnp.int32, (rows, LANES), 1) < GY


def force_stain(s_ref, k, j, regions, f_ref, u_ref, r_ref, y_ref, matrix):
    tiles = s_ref.shape[1]
    parts = [s_ref[k, :, s0 : s0 + n, :] for s0, _, _, n in regions]
    x = parts[0] if len(parts) == 1 else jnp.concatenate(parts, 1)
    total = x.shape[1]
    p = lateral(x.reshape(tiles * total, LANES), matrix)
    y_ref[...] = p[:, :LANES].reshape(tiles, total, LANES)
    r_ref[1 : tiles + 1] = p[:, LANES:].reshape(tiles, total, LANES)
    lo = low_half(16)
    for s0, f0, u0, n in regions:
        for z in range(0, n, 16):
            rows = slice(f0 + z, f0 + z + 16)
            r_now = r_ref[1, rows, :]
            before = jnp.where(lo, r_ref[0, rows, :], r_now)
            for c in range(tiles):
                r_next = r_ref[c + 2, rows, :]
                after = jnp.where(lo, r_now, r_next)
                gx = after - before
                before, r_now = after, r_next
                gy = y_ref[c, rows, :]
                s = s0 + z
                gz = s_ref[k, c, s + 1 : s + 17, :] - s_ref[k, c, s - 1 : s + 15, :]
                fixed = f_ref[j, rows, c * LANES : (c + 1) * LANES].astype(F32)
                at = slice(u0 + z, u0 + z + 16)
                ux, uy, uz = u_ref[0, c, at, :], u_ref[1, c, at, :], u_ref[2, c, at, :]
                moved = (gx * ux + gy * uy) + gz * uz
                twice = (fixed - s_ref[k, c, s : s + 16, :]) * 2.0 - moved
                denom = (gx * gx + gy * gy) + (gz * gz + (twice * twice + 2.0))
                w = twice / denom
                u_ref[0, c, at, :] = ux + w * gx
                u_ref[1, c, at, :] = uy + w * gy
                u_ref[2, c, at, :] = uz + w * gz


def sweep(src, store, q, z0, rows, r_ref, matrix):
    tiles = src.shape[1]
    x = src[q, :, z0 : z0 + rows, :].reshape(tiles * rows, LANES)
    p = lateral(x, matrix)
    r_ref[1 : tiles + 1] = p[:, LANES:].reshape(tiles, rows, LANES)
    inside = p[:, :LANES].reshape(tiles, rows, LANES)
    lo = low_half(rows)
    for c in range(tiles):
        depth = src[q, c, z0 - 1 : z0 - 1 + rows, :] + src[q, c, z0 + 1 : z0 + 1 + rows, :]
        across = jnp.where(lo, r_ref[c, :, :], r_ref[c + 2, :, :])
        store(c, src[q, c, z0 : z0 + rows, :] * (1.0 / RATE - 6.0) + depth + (inside[c] + across))


def fetch_template(own, recv, owner, k, j, f_ref, pieces, sems, base):
    mine = owner[k] == lax.axis_index("subj")
    for i, (src, dst, n) in enumerate(pieces):

        def copy(ref, i=i, src=src, dst=dst, n=n):
            return pltpu.make_async_copy(
                ref.at[0, k, pl.ds(src, n), :], f_ref.at[j, pl.ds(dst, n), :], sems.at[base + i]
            )

        @pl.when(mine)
        def _():
            copy(own).start()

        @pl.when(jnp.logical_not(mine))
        def _():
            copy(recv).start()


def wait_template(own, k, j, f_ref, pieces, sems, base):
    for i, (src, dst, n) in enumerate(pieces):
        pltpu.make_async_copy(
            own.at[0, k, pl.ds(src, n), :], f_ref.at[j, pl.ds(dst, n), :], sems.at[base + i]
        ).wait()


def edge_kernel(depth, order, owner, even_recv, odd_recv, subject, own, recv, moved, u_ref, even_send, odd_send,
                s_ref, f_ref, r_ref, y_ref, s_sem, f_sem, u_sem):
    stains, tiles = s_ref.shape[:2]
    last = depth // 8
    even = (lax.axis_index("depth") % 2) == 0
    s_copies = []
    for j in range(stains):
        for i, t in enumerate((0, 1, 2, last - 3, last - 2, last - 1)):
            s_copies.append(
                pltpu.make_async_copy(
                    subject.at[order[0, j], t], s_ref.at[order[0, j], :, 8 + 8 * i : 16 + 8 * i, :], s_sem.at[j, i]
                )
            )
    u_copies = [
        pltpu.make_async_copy(moved.at[:, t], u_ref.at[:, :, 8 * i : 8 * i + 8, :], u_sem.at[i])
        for i, t in enumerate((0, 1, last - 2, last - 1))
    ]
    pieces = ((0, 0, EDGE), (depth - EDGE, EDGE, EDGE))
    for j in range(stains):
        for copy in s_copies[6 * j : 6 * j + 6]:
            copy.start()
        fetch_template(own, recv, owner, order[0, j], j, f_ref, pieces, f_sem, 2 * j)
        if j == 0:
            for copy in u_copies:
                copy.start()
    r_ref[0] = jnp.zeros(r_ref.shape[1:], F32)
    r_ref[tiles + 1] = jnp.zeros(r_ref.shape[1:], F32)
    matrix = lateral_matrix(True)
    for c in range(tiles):
        at = slice(c * LANES, (c + 1) * LANES)
        a, b = even_recv[:, at], odd_recv[:, at]
        low, high = jnp.where(even, b, a), jnp.where(even, a, b)
        for k in range(stains):
            s_ref[k, c, 7:8, :] = low[k : k + 1]
            s_ref[k, c, 56:57, :] = high[k : k + 1]
    regions = ((8, 0, 0, EDGE), (40, EDGE, EDGE, EDGE))
    for j in range(stains):
        for copy in s_copies[6 * j : 6 * j + 6]:
            copy.wait()
        wait_template(own, order[0, j], j, f_ref, pieces, f_sem, 2 * j)
        if j == 0:
            for copy in u_copies:
                copy.wait()
        force_stain(s_ref, order[0, j], j, regions, f_ref, u_ref, r_ref, y_ref, matrix)
    n = SWEEPS
    for q in range(3):
        for c in range(tiles):
            at = slice(c * LANES, (c + 1) * LANES)
            low, high = u_ref[q, c, 0:n, :], u_ref[q, c, 2 * EDGE - n : 2 * EDGE, :]
            even_send[q, :, at] = jnp.where(even, high, low)
            odd_send[q, :, at] = jnp.where(even, low, high)


def inner_kernel(depth, order, owner, subject, own, recv, moved, edge, out,
                 s_ref, f_ref, r_ref, y_ref, a_ref, b_ref, rs_ref, o_ref, s_sem, f_sem, u_sem, o_sem):
    stains, tiles = s_ref.shape[:2]
    last = depth // 8
    first = EDGE // 8
    count = last - 2 * first
    rows = depth - 2 * EDGE
    s_copies = []
    for j in range(stains):
        k = order[0, j]
        for i in range(count + 2):
            s_copies.append(
                pltpu.make_async_copy(
                    subject.at[k, first - 1 + i], s_ref.at[k, :, 8 * i : 8 * i + 8, :], s_sem.at[j, i]
                )
            )
    per = count + 2
    u_copies = [
        pltpu.make_async_copy(
            moved.at[:, first + i], a_ref.at[:, :, 8 + EDGE + 8 * i : 16 + EDGE + 8 * i, :], u_sem.at[i]
        )
        for i in range(count)
    ]
    e_copies = [
        pltpu.make_async_copy(edge.at[:, :, 0:EDGE, :], a_ref.at[:, :, 8 : 8 + EDGE, :], u_sem.at[count]),
        pltpu.make_async_copy(
            edge.at[:, :, EDGE : 2 * EDGE, :], a_ref.at[:, :, 8 + depth - EDGE : 8 + depth, :], u_sem.at[count + 1]
        ),
    ]
    pieces = ((EDGE, 0, rows),)
    for j in range(stains):
        for copy in s_copies[per * j : per * j + per]:
            copy.start()
        fetch_template(own, recv, owner, order[0, j], j, f_ref, pieces, f_sem, j)
        if j == 0:
            for copy in u_copies:
                copy.start()
    for copy in e_copies:
        copy.start()
    for ref in (r_ref, rs_ref):
        ref[0] = jnp.zeros(ref.shape[1:], F32)
        ref[tiles + 1] = jnp.zeros(ref.shape[1:], F32)
    for ref in (a_ref, b_ref):
        ref[:, :, 0:8, :] = jnp.zeros((3, tiles, 8, LANES), F32)
        ref[:, :, 8 + depth : 16 + depth, :] = jnp.zeros((3, tiles, 8, LANES), F32)
    matrix = lateral_matrix(True)
    for j in range(stains):
        k = order[0, j]
        for copy in s_copies[per * j : per * j + per]:
            copy.wait()
        wait_template(own, k, j, f_ref, pieces, f_sem, j)
        if j == 0:
            for copy in u_copies:
                copy.wait()
        force_stain(s_ref, k, j, ((8, 0, 8 + EDGE, rows),), f_ref, a_ref, r_ref, y_ref, matrix)
    for copy in e_copies:
        copy.wait()
    matrix = lateral_matrix(False)
    src, dst = a_ref, b_ref
    for i in range(SWEEPS):
        final = i == SWEEPS - 1

        def one(q, _, src=src, dst=dst, final=final):
            def store(c, value):
                if final:
                    o_ref[q, :, c * LANES : (c + 1) * LANES] = value * RATE**SWEEPS
                else:
                    dst[q, c, 8 : 8 + depth, :] = value

            sweep(src, store, q, 8, depth, rs_ref, matrix)
            if final:
                pltpu.make_async_copy(o_ref.at[q], out.at[0, q], o_sem.at[q]).start()
            return 0

        lax.fori_loop(0, 3, one, 0)
        src, dst = dst, src
    for q in range(3):
        pltpu.make_async_copy(o_ref.at[q], out.at[0, q], o_sem.at[q]).wait()


def seam_kernel(depth, edge, even_recv, odd_recv, before, out, a_ref, b_ref, r_ref, o_ref, sem):
    tiles = edge.shape[1]
    at_depth = lax.axis_index("depth")
    even = (at_depth % 2) == 0
    has_low = at_depth > 0
    has_high = at_depth < lax.axis_size("depth") - 1
    ends = (0, depth - 8)
    ins = [
        pltpu.make_async_copy(before.at[0, :, z : z + 8, :], o_ref.at[i], sem.at[i]) for i, z in enumerate(ends)
    ]
    outs = [pltpu.make_async_copy(o_ref.at[i], out.at[0, :, z : z + 8, :], sem.at[i]) for i, z in enumerate(ends)]
    a_copies = [
        pltpu.make_async_copy(edge.at[:, :, 2 * EDGE - 8 : 2 * EDGE, :], a_ref.at[:, :, 8:16, :], sem.at[2]),
        pltpu.make_async_copy(edge.at[:, :, 0:8, :], a_ref.at[:, :, 24:32, :], sem.at[3]),
    ]
    for copy in a_copies + ins:
        copy.start()
    r_ref[0] = jnp.zeros(r_ref.shape[1:], F32)
    r_ref[tiles + 1] = jnp.zeros(r_ref.shape[1:], F32)
    for ref in (a_ref, b_ref):
        for z in (0, 32):
            ref[:, :, z : z + 8, :] = jnp.zeros((3, tiles, 8, LANES), F32)
    n = SWEEPS
    for q in range(3):
        for c in range(tiles):
            at = slice(c * LANES, (c + 1) * LANES)
            x, y = even_recv[q, :, at], odd_recv[q, :, at]
            a_ref[q, c, 16 : 16 + n, :] = jnp.where(even, x, y)
            a_ref[q, c, 20 : 20 + n, :] = jnp.where(even, y, x)
    row = lax.broadcasted_iota(jnp.int32, (24, LANES), 0)
    keep = jnp.where((row >= 8) & (row < 12), jnp.where(has_high, 1.0, 0.0), 1.0)
    keep = jnp.where((row >= 12) & (row < 16), jnp.where(has_low, 1.0, 0.0), keep)
    top = lax.broadcasted_iota(jnp.int32, (8, LANES), 0) < 4
    matrix = lateral_matrix(False)
    for copy in a_copies:
        copy.wait()
    src, dst = a_ref, b_ref
    for i in range(SWEEPS):
        final = i == SWEEPS - 1
        if final:
            for copy in ins:
                copy.wait()

        def one(q, _, src=src, dst=dst, final=final):
            def store(c, value):
                at = slice(c * LANES, (c + 1) * LANES)
                if final:
                    value = value * RATE**SWEEPS
                    o_ref[0, q, :, at] = jnp.where(top, value[16:24], o_ref[0, q, :, at])
                    o_ref[1, q, :, at] = jnp.where(top, o_ref[1, q, :, at], value[0:8])
                else:
                    dst[q, c, 8:32, :] = value * keep

            sweep(src, store, q, 8, 24, r_ref, matrix)
            return 0

        lax.fori_loop(0, 3, one, 0)
        src, dst = dst, src
    for copy in outs:
        copy.start()
    for copy in outs:
        copy.wait()


def local(template, owner, order, subject, displacement):
    stains, depth, cells = subject.shape[1:]
    tiles = cells // LANES
    count = lax.axis_size("depth")
    even_pairs, odd_pairs = pair_swaps(count)
    even = (lax.axis_index("depth") % 2) == 0

    recv = lax.ppermute(template, "subj", [(0, 1), (1, 0)])
    first, final = subject[0, :, 0, :], subject[0, :, depth - 1, :]
    even_recv = lax.ppermute(jnp.where(even, final, first), "depth", even_pairs)
    odd_recv = lax.ppermute(jnp.where(even, first, final), "depth", odd_pairs)

    def tiled(a):
        return a.reshape(a.shape[1], depth // 8, 8, tiles, LANES).transpose(0, 1, 3, 2, 4)

    subject5, moved5 = tiled(subject), tiled(displacement)
    sds = jax.ShapeDtypeStruct
    dma = pltpu.SemaphoreType.DMA
    edge, even_send, odd_send = pl.pallas_call(
        functools.partial(edge_kernel, depth),
        out_shape=(
            sds((3, tiles, 2 * EDGE, LANES), F32),
            sds((3, SWEEPS, cells), F32),
            sds((3, SWEEPS, cells), F32),
        ),
        in_specs=[SMEM, SMEM, VMEM, VMEM, ANY, ANY, ANY, ANY],
        out_specs=(VMEM, VMEM, VMEM),
        scratch_shapes=[
            pltpu.VMEM((stains, tiles, 64, LANES), F32),
            pltpu.VMEM((stains, 2 * EDGE, cells), BF16),
            pltpu.VMEM((tiles + 2, 2 * EDGE, LANES), F32),
            pltpu.VMEM((tiles, 2 * EDGE, LANES), F32),
            dma((stains, 6)),
            dma((2 * stains,)),
            dma((4,)),
        ],
        compiler_params=params(),
        cost_estimate=pl.CostEstimate(flops=10**8, bytes_accessed=8 << 20, transcendentals=0),
        name="edge_force",
    )(order, owner, even_recv, odd_recv, subject5, template, recv, moved5)

    u_even = lax.ppermute(even_send, "depth", even_pairs)
    u_odd = lax.ppermute(odd_send, "depth", odd_pairs)

    inner = depth - 2 * EDGE
    inside = pl.pallas_call(
        functools.partial(inner_kernel, depth),
        out_shape=sds(displacement.shape, F32),
        in_specs=[SMEM, SMEM, ANY, ANY, ANY, ANY, ANY],
        out_specs=ANY,
        scratch_shapes=[
            pltpu.VMEM((stains, tiles, inner + 16, LANES), F32),
            pltpu.VMEM((stains, inner, cells), BF16),
            pltpu.VMEM((tiles + 2, inner, LANES), F32),
            pltpu.VMEM((tiles, inner, LANES), F32),
            pltpu.VMEM((3, tiles, depth + 16, LANES), F32),
            pltpu.VMEM((3, tiles, depth + 16, LANES), F32),
            pltpu.VMEM((tiles + 2, depth, LANES), F32),
            pltpu.VMEM((3, depth, cells), F32),
            dma((stains, inner // 8 + 2)),
            dma((stains,)),
            dma((inner // 8 + 2,)),
            dma((3,)),
        ],
        compiler_params=params(),
        cost_estimate=pl.CostEstimate(flops=10**9, bytes_accessed=40 << 20, transcendentals=0),
        name="inner_force_and_sweeps",
    )(order, owner, subject5, template, recv, moved5, edge)

    return pl.pallas_call(
        functools.partial(seam_kernel, depth),
        out_shape=sds(displacement.shape, F32),
        in_specs=[ANY, VMEM, VMEM, ANY],
        out_specs=ANY,
        scratch_shapes=[
            pltpu.VMEM((3, tiles, 40, LANES), F32),
            pltpu.VMEM((3, tiles, 40, LANES), F32),
            pltpu.VMEM((tiles + 2, 24, LANES), F32),
            pltpu.VMEM((2, 3, 8, cells), F32),
            dma((4,)),
        ],
        input_output_aliases={3: 0},
        compiler_params=params(),
        name="seam_sweeps",
    )(edge, u_even, u_odd, inside)


def solution(mesh):
    placed = (
        P("subj", None, "depth", None),
        P(),
        P(("grp", "subj"), None),
        P(("grp", "subj"), None, "depth", None),
        P(("grp", "subj"), None, "depth", None),
    )
    return jax.shard_map(
        local,
        mesh=mesh,
        in_specs=placed,
        out_specs=P(("grp", "subj"), None, "depth", None),
        check_vma=False,
    )
```

```python
import functools

import jax
import jax.numpy as jnp
from jax import lax
from jax.experimental import pallas as pl
from jax.experimental.pallas import tpu as pltpu
from jax.sharding import PartitionSpec as P

GY = 64
SWEEPS = 4
LANES = 128
RATE = 0.15
F32 = jnp.float32
BF16 = jnp.bfloat16

ANY = pl.BlockSpec(memory_space=pl.ANY)
HBM = pl.BlockSpec(memory_space=pltpu.HBM)
VMEM = pl.BlockSpec(memory_space=pltpu.VMEM)


def params(mib):
    return pltpu.CompilerParams(vmem_limit_bytes=mib << 20)


def pair_swaps(count):
    def swaps(first):
        return [p for i in range(first, count - 1, 2) for p in ((i, i + 1), (i + 1, i))]

    return swaps(0), swaps(1)


def lateral_matrix(difference):
    row = lax.broadcasted_iota(jnp.int32, (2 * LANES, 2 * LANES), 0) & (LANES - 1)
    col = lax.broadcasted_iota(jnp.int32, (2 * LANES, 2 * LANES), 1)
    right = col >= LANES
    col = col & (LANES - 1)
    swap = jnp.where((row ^ col) == GY, 1.0, 0.0)
    same = (row & GY) == (col & GY)
    plus = jnp.where((row == col + 1) & same, 1.0, 0.0)
    minus = jnp.where((row == col - 1) & same, 1.0, 0.0)
    left = plus - minus if difference else plus + minus + swap
    return jnp.where(right, swap, left).astype(BF16)


def lateral(x, matrix):
    high = x.astype(BF16)
    low = (x - high.astype(F32)).astype(BF16)
    return jnp.dot(jnp.concatenate([high, low], 1), matrix, preferred_element_type=F32)


def low_half(rows):
    return lax.broadcasted_iota(jnp.int32, (rows, LANES), 1) < GY


def pieces_of(start, rows):
    done = start
    while done < start + rows:
        block = done // 16 * 16
        stop = min(block + 16, start + rows)
        yield block, done - block, stop - done
        done = stop


def force_stain(s_ref, k, regions, f_ref, u_ref, r_ref, y_ref, matrix):
    tiles = s_ref.shape[1]
    parts = [s_ref[k, :, s0 : s0 + n, :] for s0, _, _, n in regions]
    x = parts[0] if len(parts) == 1 else jnp.concatenate(parts, 1)
    total = x.shape[1]
    p = lateral(x.reshape(tiles * total, LANES), matrix)
    y_ref[...] = p[:, :LANES].reshape(tiles, total, LANES)
    r_ref[1 : tiles + 1] = p[:, LANES:].reshape(tiles, total, LANES)
    base = 0
    for s0, f0, u0, n in regions:
        for block, skip, count in pieces_of(f0, n):
            z = block + skip - f0
            rows = slice(base + z, base + z + count)
            at = slice(u0 + z, u0 + z + count)
            s = s0 + z
            lo = low_half(count)
            r_now = r_ref[1, rows, :]
            before = jnp.where(lo, r_ref[0, rows, :], r_now)
            for c in range(tiles):
                r_next = r_ref[c + 2, rows, :]
                after = jnp.where(lo, r_now, r_next)
                gx = after - before
                before, r_now = after, r_next
                gy = y_ref[c, rows, :]
                gz = s_ref[k, c, s + 1 : s + 1 + count, :] - s_ref[k, c, s - 1 : s - 1 + count, :]
                fixed = f_ref[k, block : block + 16, c * LANES : (c + 1) * LANES].astype(F32)
                fixed = fixed[skip : skip + count]
                ux, uy, uz = u_ref[0, c, at, :], u_ref[1, c, at, :], u_ref[2, c, at, :]
                moved = (gx * ux + gy * uy) + gz * uz
                twice = (fixed - s_ref[k, c, s : s + count, :]) * 2.0 - moved
                denom = (gx * gx + gy * gy) + (gz * gz + (twice * twice + 2.0))
                w = twice * inverse(denom)
                u_ref[0, c, at, :] = ux + w * gx
                u_ref[1, c, at, :] = uy + w * gy
                u_ref[2, c, at, :] = uz + w * gz
        base += n


def inverse(x):
    r = pl.reciprocal(x, approx=True)
    return r * (2.0 - x * r)


def sweep(src, store, q, z0, rows, r_ref, matrix):
    tiles = src.shape[1]
    x = src[q, :, z0 : z0 + rows, :].reshape(tiles * rows, LANES)
    p = lateral(x, matrix)
    r_ref[q, 1 : tiles + 1] = p[:, LANES:].reshape(tiles, rows, LANES)
    inside = p[:, :LANES].reshape(tiles, rows, LANES)
    lo = low_half(rows)
    for c in range(tiles):
        depth = src[q, c, z0 - 1 : z0 - 1 + rows, :] + src[q, c, z0 + 1 : z0 + 1 + rows, :]
        across = jnp.where(lo, r_ref[q, c, :, :], r_ref[q, c + 2, :, :])
        store(c, src[q, c, z0 : z0 + rows, :] * (1.0 / RATE - 6.0) + depth + (inside[c] + across))


def clear_rim(ref, axis):
    shape = list(ref.shape)
    shape[axis] = 1
    at = [slice(None)] * len(shape)
    for i in (0, ref.shape[axis] - 1):
        at[axis] = slice(i, i + 1)
        ref[tuple(at)] = jnp.zeros(shape, F32)


class Template:
    def __init__(self, own, recv, owner, f_ref, sems, pieces):
        self.own, self.recv, self.owner, self.f_ref, self.sems, self.pieces = own, recv, owner, f_ref, sems, pieces

    def copy(self, ref, k, i):
        src, dst, n = self.pieces[i]
        return pltpu.make_async_copy(
            ref.at[0, k, pl.ds(src, n), :], self.f_ref.at[k, pl.ds(dst, n), :], self.sems.at[k, i]
        )

    def start(self, k):
        mine = self.owner[k] == lax.axis_index("subj")

        @pl.when(mine)
        def _():
            for i in range(len(self.pieces)):
                self.copy(self.own, k, i).start()

        @pl.when(jnp.logical_not(mine))
        def _():
            for i in range(len(self.pieces)):
                self.copy(self.recv, k, i).start()

    def wait(self, k):
        for i in range(len(self.pieces)):
            self.copy(self.own, k, i).wait()


def force_steps(order_hbm, owner_hbm, subject, own, recv, moved, order, owner, s_ref, f_ref, r_ref, y_ref,
                u_ref, o_sem, s_sem, f_sem, u_sem, planes, pieces, u_planes, regions, halo=None):
    stains = s_ref.shape[0]
    small = [
        pltpu.make_async_copy(order_hbm, order, o_sem.at[0]),
        pltpu.make_async_copy(owner_hbm, owner, o_sem.at[1]),
    ]
    for copy in small:
        copy.start()

    def s_copies(k):
        return [
            pltpu.make_async_copy(subject.at[k, t], s_ref.at[k, :, z : z + 8, :], s_sem.at[k, i])
            for i, (t, z) in enumerate(planes)
        ]

    for copy in small:
        copy.wait()
    template = Template(own, recv, owner, f_ref, f_sem, pieces)
    u_copies = [
        pltpu.make_async_copy(moved.at[:, t], u_ref.at[:, :, z : z + 8, :], u_sem.at[i])
        for i, (t, z) in enumerate(u_planes)
    ]
    for j in range(stains):
        k = order[0, j]
        for copy in s_copies(k):
            copy.start()
        template.start(k)
        if j == 0:
            for copy in u_copies:
                copy.start()
    clear_rim(r_ref, 0)
    matrix = lateral_matrix(True)
    if halo is not None:
        halo()
    for j in range(stains):
        k = order[0, j]
        for copy in s_copies(k):
            copy.wait()
        template.wait(k)
        if j == 0:
            for copy in u_copies:
                copy.wait()
        force_stain(s_ref, k, regions, f_ref, u_ref, r_ref, y_ref, matrix)


def inner_kernel(depth, order_hbm, owner_hbm, subject, own, recv, moved, u_ref, *scratch):
    last = depth // 8
    planes = [(t, 8 * t) for t in range(last)]
    u_planes = [(t, 8 * t - 8) for t in range(1, last - 1)]
    order, owner, s_ref, f_ref, r_ref, y_ref, o_sem, s_sem, f_sem, u_sem = scratch
    force_steps(order_hbm, owner_hbm, subject, own, recv, moved, order, owner, s_ref, f_ref, r_ref, y_ref,
                u_ref, o_sem, s_sem, f_sem, u_sem, planes, ((0, 0, depth),), u_planes, ((8, 8, 0, depth - 16),))


def edge_kernel(depth, order_hbm, owner_hbm, even_recv, odd_recv, subject, own, recv, moved, middle, u_ref, even_send,
                odd_send, *scratch):
    order, owner, s_ref, f_ref, r_ref, y_ref, o_sem, s_sem, f_sem, u_sem = scratch
    stains, tiles = s_ref.shape[:2]
    last = depth // 8
    even = (lax.axis_index("depth") % 2) == 0

    def halo():
        for c in range(tiles):
            at = slice(c * LANES, (c + 1) * LANES)
            a, b = even_recv[:, at], odd_recv[:, at]
            low, high = jnp.where(even, b, a), jnp.where(even, a, b)
            for k in range(stains):
                s_ref[k, c, 7:8, :] = low[k : k + 1]
                s_ref[k, c, 40:41, :] = high[k : k + 1]

    planes = [(0, 8), (1, 16), (last - 2, 24), (last - 1, 32)]
    pieces = ((0, 0, 16), (depth - 16, 16, 16))
    force_steps(order_hbm, owner_hbm, subject, own, recv, moved, order, owner, s_ref, f_ref, r_ref, y_ref,
                u_ref, o_sem, s_sem, f_sem, u_sem, planes, pieces, [(0, 0), (last - 1, 8)],
                ((8, 0, 0, 8), (32, 24, 8, 8)), halo)
    n = SWEEPS
    for q in range(3):
        for c in range(tiles):
            at = slice(c * LANES, (c + 1) * LANES)
            low, high = u_ref[q, c, 0:n, :], u_ref[q, c, 16 - n : 16, :]
            even_send[q, :, at] = jnp.where(even, high, low)
            odd_send[q, :, at] = jnp.where(even, low, high)


def sweep_kernel(depth, middle, edge, out, a_ref, b_ref, r_ref, o_ref, sem, o_sem):
    tiles = a_ref.shape[1]

    def ins(q):
        return [
            pltpu.make_async_copy(middle.at[q], a_ref.at[q, :, 16:depth, :], sem.at[q, 0]),
            pltpu.make_async_copy(edge.at[q, :, 0:8, :], a_ref.at[q, :, 8:16, :], sem.at[q, 1]),
            pltpu.make_async_copy(edge.at[q, :, 8:16, :], a_ref.at[q, :, depth : depth + 8, :], sem.at[q, 2]),
        ]

    for q in range(3):
        for copy in ins(q):
            copy.start()
    clear_rim(r_ref, 1)
    for ref in (a_ref, b_ref):
        for z in (0, depth + 8):
            ref[:, :, z : z + 8, :] = jnp.zeros((3, tiles, 8, LANES), F32)
    matrix = lateral_matrix(False)
    src, dst = a_ref, b_ref
    for i in range(SWEEPS):
        final = i == SWEEPS - 1
        for q in range(3):

            def store(c, value, q=q, dst=dst, final=final):
                if final:
                    o_ref[q, :, c * LANES : (c + 1) * LANES] = value * RATE**SWEEPS
                else:
                    dst[q, c, 8 : 8 + depth, :] = value

            if i == 0:
                for copy in ins(q):
                    copy.wait()
            sweep(src, store, q, 8, depth, r_ref, matrix)
            if final:
                pltpu.make_async_copy(o_ref.at[q], out.at[0, q], o_sem.at[q]).start()
        src, dst = dst, src
    for q in range(3):
        pltpu.make_async_copy(o_ref.at[q], out.at[0, q], o_sem.at[q]).wait()


def seam_kernel(depth, edge, even_recv, odd_recv, before, out, a_ref, b_ref, r_ref, o_ref, sem):
    tiles = edge.shape[1]
    at_depth = lax.axis_index("depth")
    even = (at_depth % 2) == 0
    has_low = at_depth > 0
    has_high = at_depth < lax.axis_size("depth") - 1
    ends = (0, depth - 8)
    ins = [
        pltpu.make_async_copy(before.at[0, :, z : z + 8, :], o_ref.at[i], sem.at[i]) for i, z in enumerate(ends)
    ]
    outs = [pltpu.make_async_copy(o_ref.at[i], out.at[0, :, z : z + 8, :], sem.at[i]) for i, z in enumerate(ends)]
    a_copies = [
        pltpu.make_async_copy(edge.at[:, :, 8:16, :], a_ref.at[:, :, 8:16, :], sem.at[2]),
        pltpu.make_async_copy(edge.at[:, :, 0:8, :], a_ref.at[:, :, 24:32, :], sem.at[3]),
    ]
    for copy in a_copies + ins:
        copy.start()
    clear_rim(r_ref, 1)
    for ref in (a_ref, b_ref):
        for z in (0, 32):
            ref[:, :, z : z + 8, :] = jnp.zeros((3, tiles, 8, LANES), F32)
    n = SWEEPS
    for q in range(3):
        for c in range(tiles):
            at = slice(c * LANES, (c + 1) * LANES)
            x, y = even_recv[q, :, at], odd_recv[q, :, at]
            a_ref[q, c, 16 : 16 + n, :] = jnp.where(even, x, y)
            a_ref[q, c, 20 : 20 + n, :] = jnp.where(even, y, x)
    row = lax.broadcasted_iota(jnp.int32, (24, LANES), 0)
    keep = jnp.where((row >= 8) & (row < 12), jnp.where(has_high, 1.0, 0.0), 1.0)
    keep = jnp.where((row >= 12) & (row < 16), jnp.where(has_low, 1.0, 0.0), keep)
    top = lax.broadcasted_iota(jnp.int32, (8, LANES), 0) < 4
    matrix = lateral_matrix(False)
    for copy in a_copies:
        copy.wait()
    src, dst = a_ref, b_ref
    for i in range(SWEEPS):
        final = i == SWEEPS - 1
        if final:
            for copy in ins:
                copy.wait()
        for q in range(3):

            def store(c, value, q=q, dst=dst, final=final):
                at = slice(c * LANES, (c + 1) * LANES)
                if final:
                    value = value * RATE**SWEEPS
                    o_ref[0, q, :, at] = jnp.where(top, value[16:24], o_ref[0, q, :, at])
                    o_ref[1, q, :, at] = jnp.where(top, o_ref[1, q, :, at], value[0:8])
                else:
                    dst[q, c, 8:32, :] = value * keep

            sweep(src, store, q, 8, 24, r_ref, matrix)
        src, dst = dst, src
    for copy in outs:
        copy.start()
    for copy in outs:
        copy.wait()


def local(template, owner, order, subject, displacement):
    stains, depth, cells = subject.shape[1:]
    tiles = cells // LANES
    count = lax.axis_size("depth")
    even_pairs, odd_pairs = pair_swaps(count)
    even = (lax.axis_index("depth") % 2) == 0

    recv = lax.ppermute(template, "subj", [(0, 1), (1, 0)])
    first, final = subject[0, :, 0, :], subject[0, :, depth - 1, :]
    even_recv = lax.ppermute(jnp.where(even, final, first), "depth", even_pairs)
    odd_recv = lax.ppermute(jnp.where(even, first, final), "depth", odd_pairs)

    def tiled(a):
        return a.reshape(a.shape[1], depth // 8, 8, tiles, LANES).transpose(0, 1, 3, 2, 4)

    subject5, moved5 = tiled(subject), tiled(displacement)
    sds = jax.ShapeDtypeStruct
    dma = pltpu.SemaphoreType.DMA

    def force_scratch(s_planes, f_planes, planes, s_parts, f_parts, u_parts):
        return [
            pltpu.SMEM(order.shape, jnp.int32),
            pltpu.SMEM(owner.shape, jnp.int32),
            pltpu.VMEM((stains, tiles, s_planes, LANES), F32),
            pltpu.VMEM((stains, f_planes, cells), BF16),
            pltpu.VMEM((tiles + 2, planes, LANES), F32),
            pltpu.VMEM((tiles, planes, LANES), F32),
            dma((2,)),
            dma((stains, s_parts)),
            dma((stains, f_parts)),
            dma((u_parts,)),
        ]

    tall = depth // 8
    middle = pl.pallas_call(
        functools.partial(inner_kernel, depth),
        out_shape=sds((3, tiles, depth - 16, LANES), F32),
        in_specs=[HBM] * 6,
        out_specs=VMEM,
        scratch_shapes=force_scratch(depth, depth, depth - 16, tall, 1, tall - 2),
        compiler_params=params(64),
        cost_estimate=pl.CostEstimate(flops=4 * 10**8, bytes_accessed=10 << 20, transcendentals=0),
        name="inner_force",
    )(order, owner, subject5, template, recv, moved5)

    edge, even_send, odd_send = pl.pallas_call(
        functools.partial(edge_kernel, depth),
        out_shape=(
            sds((3, tiles, 16, LANES), F32),
            sds((3, SWEEPS, cells), F32),
            sds((3, SWEEPS, cells), F32),
        ),
        in_specs=[HBM, HBM, VMEM, VMEM, HBM, HBM, HBM, HBM, ANY],
        out_specs=(VMEM, VMEM, VMEM),
        scratch_shapes=force_scratch(48, 32, 16, 4, 2, 2),
        compiler_params=params(64),
        cost_estimate=pl.CostEstimate(flops=10**8, bytes_accessed=8 << 20, transcendentals=0),
        name="edge_force",
    )(order, owner, even_recv, odd_recv, subject5, template, recv, moved5, middle)

    u_even = lax.ppermute(even_send, "depth", even_pairs)
    u_odd = lax.ppermute(odd_send, "depth", odd_pairs)

    inside = pl.pallas_call(
        functools.partial(sweep_kernel, depth),
        out_shape=sds(displacement.shape, F32),
        in_specs=[ANY, ANY],
        out_specs=ANY,
        scratch_shapes=[
            pltpu.VMEM((3, tiles, depth + 16, LANES), F32),
            pltpu.VMEM((3, tiles, depth + 16, LANES), F32),
            pltpu.VMEM((3, tiles + 2, depth, LANES), F32),
            pltpu.VMEM((3, depth, cells), F32),
            dma((3, 3)),
            dma((3,)),
        ],
        compiler_params=params(64),
        cost_estimate=pl.CostEstimate(flops=10**9, bytes_accessed=40 << 20, transcendentals=0),
        name="sweeps",
    )(middle, edge)

    return pl.pallas_call(
        functools.partial(seam_kernel, depth),
        out_shape=sds(displacement.shape, F32),
        in_specs=[ANY, VMEM, VMEM, ANY],
        out_specs=ANY,
        scratch_shapes=[
            pltpu.VMEM((3, tiles, 40, LANES), F32),
            pltpu.VMEM((3, tiles, 40, LANES), F32),
            pltpu.VMEM((3, tiles + 2, 24, LANES), F32),
            pltpu.VMEM((2, 3, 8, cells), F32),
            dma((4,)),
        ],
        input_output_aliases={3: 0},
        compiler_params=params(64),
        name="seam_sweeps",
    )(edge, u_even, u_odd, inside)


def solution(mesh):
    placed = (
        P("subj", None, "depth", None),
        P(),
        P(("grp", "subj"), None),
        P(("grp", "subj"), None, "depth", None),
        P(("grp", "subj"), None, "depth", None),
    )
    return jax.shard_map(
        local,
        mesh=mesh,
        in_specs=placed,
        out_specs=P(("grp", "subj"), None, "depth", None),
        check_vma=False,
    )
```

```python
import functools

import jax
import jax.numpy as jnp
from jax import lax
from jax.experimental import pallas as pl
from jax.experimental.pallas import tpu as pltpu
from jax.sharding import PartitionSpec as P

GY = 64
SWEEPS = 4
LANES = 128
RATE = 0.15
F32 = jnp.float32
BF16 = jnp.bfloat16
LIMIT = 48
LOAD = 46

ANY = pl.BlockSpec(memory_space=pl.ANY)
HBM = pl.BlockSpec(memory_space=pltpu.HBM)
VMEM = pl.BlockSpec(memory_space=pltpu.VMEM)


def params(mib):
    return pltpu.CompilerParams(vmem_limit_bytes=mib << 20)


def pair_swaps(count):
    def swaps(first):
        return [p for i in range(first, count - 1, 2) for p in ((i, i + 1), (i + 1, i))]

    return swaps(0), swaps(1)


def lateral_matrix(difference):
    row = lax.broadcasted_iota(jnp.int32, (2 * LANES, 2 * LANES), 0) & (LANES - 1)
    col = lax.broadcasted_iota(jnp.int32, (2 * LANES, 2 * LANES), 1)
    right = col >= LANES
    col = col & (LANES - 1)
    swap = jnp.where((row ^ col) == GY, 1.0, 0.0)
    same = (row & GY) == (col & GY)
    plus = jnp.where((row == col + 1) & same, 1.0, 0.0)
    minus = jnp.where((row == col - 1) & same, 1.0, 0.0)
    left = plus - minus if difference else plus + minus + swap
    return jnp.where(right, swap, left).astype(BF16)


def lateral(x, matrix):
    high = x.astype(BF16)
    low = (x - high.astype(F32)).astype(BF16)
    return jnp.dot(jnp.concatenate([high, low], 1), matrix, preferred_element_type=F32)


def low_half(rows):
    return lax.broadcasted_iota(jnp.int32, (rows, LANES), 1) < GY


def pieces_of(start, rows):
    done = start
    while done < start + rows:
        block = done // 16 * 16
        stop = min(block + 16, start + rows)
        yield block, done - block, stop - done
        done = stop


def force_stain(s_ref, k, regions, f_ref, u_ref, r_ref, y_ref, matrix):
    tiles = s_ref.shape[1]
    parts = [s_ref[k, :, s0 : s0 + n, :] for s0, _, _, n in regions]
    x = parts[0] if len(parts) == 1 else jnp.concatenate(parts, 1)
    total = x.shape[1]
    p = lateral(x.reshape(tiles * total, LANES), matrix)
    y_ref[...] = p[:, :LANES].reshape(tiles, total, LANES)
    r_ref[1 : tiles + 1] = p[:, LANES:].reshape(tiles, total, LANES)
    base = 0
    for s0, f0, u0, n in regions:
        for block, skip, count in pieces_of(f0, n):
            z = block + skip - f0
            rows = slice(base + z, base + z + count)
            at = slice(u0 + z, u0 + z + count)
            s = s0 + z
            lo = low_half(count)
            r_now = r_ref[1, rows, :]
            before = jnp.where(lo, r_ref[0, rows, :], r_now)
            for c in range(tiles):
                r_next = r_ref[c + 2, rows, :]
                after = jnp.where(lo, r_now, r_next)
                gx = after - before
                before, r_now = after, r_next
                gy = y_ref[c, rows, :]
                gz = s_ref[k, c, s + 1 : s + 1 + count, :] - s_ref[k, c, s - 1 : s - 1 + count, :]
                fixed = f_ref[k, block : block + 16, c * LANES : (c + 1) * LANES].astype(F32)
                fixed = fixed[skip : skip + count]
                ux, uy, uz = u_ref[0, c, at, :], u_ref[1, c, at, :], u_ref[2, c, at, :]
                moved = (gx * ux + gy * uy) + gz * uz
                twice = (fixed - s_ref[k, c, s : s + count, :]) * 2.0 - moved
                denom = (gx * gx + gy * gy) + (gz * gz + (twice * twice + 2.0))
                w = twice * inverse(denom)
                u_ref[0, c, at, :] = ux + w * gx
                u_ref[1, c, at, :] = uy + w * gy
                u_ref[2, c, at, :] = uz + w * gz
        base += n


def inverse(x):
    r = pl.reciprocal(x, approx=True)
    return r * (2.0 - x * r)


def sweep(src, store, q, z0, rows, r_ref, matrix):
    tiles = src.shape[1]
    x = src[q, :, z0 : z0 + rows, :].reshape(tiles * rows, LANES)
    p = lateral(x, matrix)
    r_ref[q, 1 : tiles + 1] = p[:, LANES:].reshape(tiles, rows, LANES)
    inside = p[:, :LANES].reshape(tiles, rows, LANES)
    lo = low_half(rows)
    for c in range(tiles):
        depth = src[q, c, z0 - 1 : z0 - 1 + rows, :] + src[q, c, z0 + 1 : z0 + 1 + rows, :]
        across = jnp.where(lo, r_ref[q, c, :, :], r_ref[q, c + 2, :, :])
        store(c, src[q, c, z0 : z0 + rows, :] * (1.0 / RATE - 6.0) + depth + (inside[c] + across))


def clear_rim(ref, axis):
    shape = list(ref.shape)
    shape[axis] = 1
    at = [slice(None)] * len(shape)
    for i in (0, ref.shape[axis] - 1):
        at[axis] = slice(i, i + 1)
        ref[tuple(at)] = jnp.zeros(shape, F32)


def load_kernel(depth, subject, moved, own, s_ref, u_ref, own_ref, even_send, odd_send, s_sem, u_sem, o_sem):
    stains, tiles = s_ref.shape[:2]
    tall = depth // 8
    even = (lax.axis_index("depth") % 2) == 0

    def s_copy(t):
        return pltpu.make_async_copy(subject.at[:, t], s_ref.at[:, :, 8 + 8 * t : 16 + 8 * t, :], s_sem.at[t])

    def u_copy(t):
        return pltpu.make_async_copy(moved.at[:, t], u_ref.at[:, :, 8 + 8 * t : 16 + 8 * t, :], u_sem.at[t])

    order = (0, tall - 1) + tuple(range(1, tall - 1))
    for t in order:
        s_copy(t).start()
    for t in range(tall):
        u_copy(t).start()
    template = pltpu.make_async_copy(own.at[0], own_ref, o_sem)
    template.start()
    for z in (0, depth + 8):
        u_ref[:, :, z : z + 8, :] = jnp.zeros((3, tiles, 8, LANES), F32)
    for t in order[:2]:
        s_copy(t).wait()
    for k in range(stains):
        for c in range(tiles):
            at = slice(c * LANES, (c + 1) * LANES)
            low, high = s_ref[k, c, 8:9, :], s_ref[k, c, depth + 7 : depth + 8, :]
            even_send[k : k + 1, at] = jnp.where(even, high, low)
            odd_send[k : k + 1, at] = jnp.where(even, low, high)
    for t in order[2:]:
        s_copy(t).wait()
    for t in range(tall):
        u_copy(t).wait()
    template.wait()


def inner_kernel(depth, order_hbm, owner_hbm, s_ref, u_in, own, recv, f_ref, u_ref, order, owner, r_ref,
                 y_ref, o_sem, f_sem):
    stains = s_ref.shape[0]
    small = [
        pltpu.make_async_copy(order_hbm, order, o_sem.at[0]),
        pltpu.make_async_copy(owner_hbm, owner, o_sem.at[1]),
    ]
    for copy in small:
        copy.start()
    clear_rim(r_ref, 0)
    matrix = lateral_matrix(True)
    for copy in small:
        copy.wait()

    def f_copy(source, k):
        return pltpu.make_async_copy(source, f_ref.at[k], f_sem.at[k])

    for j in range(stains):
        k = order[0, j]
        mine = owner[k] == lax.axis_index("subj")

        @pl.when(mine)
        def _():
            f_copy(own.at[k], k).start()

        @pl.when(jnp.logical_not(mine))
        def _():
            f_copy(recv.at[0, k], k).start()

    for j in range(stains):
        k = order[0, j]
        f_copy(own.at[k], k).wait()
        force_stain(s_ref, k, ((16, 8, 16, depth - 16),), f_ref, u_ref, r_ref, y_ref, matrix)


def edge_kernel(depth, order_hbm, even_recv, odd_recv, s_in, f_ref, u_in, s_ref, u_ref, even_send, odd_send,
                order, r_ref, y_ref, o_sem):
    stains, tiles = s_ref.shape[:2]
    copy = pltpu.make_async_copy(order_hbm, order, o_sem)
    copy.start()
    even = (lax.axis_index("depth") % 2) == 0
    clear_rim(r_ref, 0)
    matrix = lateral_matrix(True)
    for c in range(tiles):
        at = slice(c * LANES, (c + 1) * LANES)
        a, b = even_recv[:, at], odd_recv[:, at]
        low, high = jnp.where(even, b, a), jnp.where(even, a, b)
        for k in range(stains):
            s_ref[k, c, 7:8, :] = low[k : k + 1]
            s_ref[k, c, depth + 8 : depth + 9, :] = high[k : k + 1]
    copy.wait()
    for j in range(stains):
        regions = ((8, 0, 8, 8), (depth, depth - 8, depth, 8))
        force_stain(s_ref, order[0, j], regions, f_ref, u_ref, r_ref, y_ref, matrix)
    n = SWEEPS
    for q in range(3):
        for c in range(tiles):
            at = slice(c * LANES, (c + 1) * LANES)
            low, high = u_ref[q, c, 8 : 8 + n, :], u_ref[q, c, 8 + depth - n : 8 + depth, :]
            even_send[q, :, at] = jnp.where(even, high, low)
            odd_send[q, :, at] = jnp.where(even, low, high)


def sweep_kernel(depth, u_ref, out, a_ref, b_ref, r_ref, o_ref, o_sem):
    tiles = a_ref.shape[1]
    clear_rim(r_ref, 1)
    for ref in (a_ref, b_ref):
        for z in (0, depth + 8):
            ref[:, :, z : z + 8, :] = jnp.zeros((3, tiles, 8, LANES), F32)
    matrix = lateral_matrix(False)
    src, dst = u_ref, a_ref
    for i in range(SWEEPS):
        final = i == SWEEPS - 1
        for q in range(3):

            def store(c, value, q=q, dst=dst, final=final):
                if final:
                    o_ref[q, :, c * LANES : (c + 1) * LANES] = value * RATE**SWEEPS
                else:
                    dst[q, c, 8 : 8 + depth, :] = value

            sweep(src, store, q, 8, depth, r_ref, matrix)
            if final:
                pltpu.make_async_copy(o_ref.at[q], out.at[0, q], o_sem.at[q]).start()
        src, dst = dst, (b_ref if dst is a_ref else a_ref)
    for q in range(3):
        pltpu.make_async_copy(o_ref.at[q], out.at[0, q], o_sem.at[q]).wait()


def seam_kernel(depth, u_ref, even_recv, odd_recv, before, out, a_ref, b_ref, r_ref, o_ref, sem):
    tiles = u_ref.shape[1]
    at_depth = lax.axis_index("depth")
    even = (at_depth % 2) == 0
    has_low = at_depth > 0
    has_high = at_depth < lax.axis_size("depth") - 1
    ends = (0, depth - 8)
    ins = [
        pltpu.make_async_copy(before.at[0, :, z : z + 8, :], o_ref.at[i], sem.at[i]) for i, z in enumerate(ends)
    ]
    outs = [
        pltpu.make_async_copy(o_ref.at[i, q], out.at[0, q, z : z + 8, :], sem.at[2 + 2 * q + i])
        for q in range(3)
        for i, z in enumerate(ends)
    ]
    for copy in ins:
        copy.start()
    clear_rim(r_ref, 1)
    n = SWEEPS
    for q in range(3):
        for ref in (a_ref, b_ref):
            for z in (0, 32):
                ref[q, :, z : z + 8, :] = jnp.zeros((tiles, 8, LANES), F32)
        a_ref[q, :, 8:16, :] = u_ref[q, :, depth : depth + 8, :]
        a_ref[q, :, 24:32, :] = u_ref[q, :, 8:16, :]
        for c in range(tiles):
            at = slice(c * LANES, (c + 1) * LANES)
            x, y = even_recv[q, :, at], odd_recv[q, :, at]
            a_ref[q, c, 16 : 16 + n, :] = jnp.where(even, x, y)
            a_ref[q, c, 20 : 20 + n, :] = jnp.where(even, y, x)
    row = lax.broadcasted_iota(jnp.int32, (24, LANES), 0)
    keep = jnp.where((row >= 8) & (row < 12), jnp.where(has_high, 1.0, 0.0), 1.0)
    keep = jnp.where((row >= 12) & (row < 16), jnp.where(has_low, 1.0, 0.0), keep)
    top = lax.broadcasted_iota(jnp.int32, (8, LANES), 0) < 4
    matrix = lateral_matrix(False)
    src, dst = a_ref, b_ref
    for i in range(SWEEPS):
        final = i == SWEEPS - 1
        if final:
            for copy in ins:
                copy.wait()
        for q in range(3):

            def store(c, value, q=q, dst=dst, final=final):
                at = slice(c * LANES, (c + 1) * LANES)
                if final:
                    value = value * RATE**SWEEPS
                    o_ref[0, q, :, at] = jnp.where(top, value[16:24], o_ref[0, q, :, at])
                    o_ref[1, q, :, at] = jnp.where(top, o_ref[1, q, :, at], value[0:8])
                else:
                    dst[q, c, 8:32, :] = value * keep

            sweep(src, store, q, 8, 24, r_ref, matrix)
            if final:
                for copy in outs[2 * q : 2 * q + 2]:
                    copy.start()
        src, dst = dst, src
    for copy in outs:
        copy.wait()


def local(template, owner, order, subject, displacement):
    stains, depth, cells = subject.shape[1:]
    tiles = cells // LANES
    count = lax.axis_size("depth")
    even_pairs, odd_pairs = pair_swaps(count)

    recv = lax.ppermute(template, "subj", [(0, 1), (1, 0)])

    def tiled(a):
        return a.reshape(a.shape[1], depth // 8, 8, tiles, LANES).transpose(0, 1, 3, 2, 4)

    subject5, moved5 = tiled(subject), tiled(displacement)
    sds = jax.ShapeDtypeStruct
    dma = pltpu.SemaphoreType.DMA

    tall = depth // 8
    s_type = pltpu.VMEM((stains, tiles, depth + 16, LANES), F32)
    f_type = pltpu.VMEM((stains, depth, cells), BF16)
    u_type = pltpu.VMEM((3, tiles, depth + 16, LANES), F32)
    send_type = pltpu.VMEM((3, SWEEPS, cells), F32)

    def force_scratch(planes):
        return [pltpu.VMEM((tiles + 2, planes, LANES), F32), pltpu.VMEM((tiles, planes, LANES), F32)]

    plane_type = pltpu.VMEM((stains, cells), F32)
    s, u, own, even_send, odd_send = pl.pallas_call(
        functools.partial(load_kernel, depth),
        out_shape=(s_type, u_type, f_type, plane_type, plane_type),
        in_specs=[HBM] * 3,
        out_specs=(VMEM,) * 5,
        scratch_shapes=[dma((tall,)), dma((tall,)), dma],
        compiler_params=params(LOAD),
        name="load",
    )(subject5, moved5, template)

    even_recv = lax.ppermute(even_send, "depth", even_pairs)
    odd_recv = lax.ppermute(odd_send, "depth", odd_pairs)

    f, u = pl.pallas_call(
        functools.partial(inner_kernel, depth),
        out_shape=(f_type, u_type),
        in_specs=[HBM, HBM, VMEM, VMEM, VMEM, ANY],
        out_specs=(VMEM, VMEM),
        scratch_shapes=[pltpu.SMEM(order.shape, jnp.int32), pltpu.SMEM(owner.shape, jnp.int32)]
        + force_scratch(depth - 16)
        + [dma((2,)), dma((stains,))],
        input_output_aliases={3: 1},
        compiler_params=params(20),
        cost_estimate=pl.CostEstimate(flops=4 * 10**8, bytes_accessed=10 << 20, transcendentals=0),
        name="inner_force",
    )(order, owner, s, u, own, recv)

    s, u, even_send, odd_send = pl.pallas_call(
        functools.partial(edge_kernel, depth),
        out_shape=(s_type, u_type, send_type, send_type),
        in_specs=[HBM, VMEM, VMEM, VMEM, VMEM, VMEM],
        out_specs=(VMEM, VMEM, VMEM, VMEM),
        scratch_shapes=[pltpu.SMEM(order.shape, jnp.int32)] + force_scratch(16) + [dma],
        input_output_aliases={3: 0, 5: 1},
        compiler_params=params(20),
        cost_estimate=pl.CostEstimate(flops=10**8, bytes_accessed=8 << 20, transcendentals=0),
        name="edge_force",
    )(order, even_recv, odd_recv, s, f, u)

    u_even = lax.ppermute(even_send, "depth", even_pairs)
    u_odd = lax.ppermute(odd_send, "depth", odd_pairs)

    inside = pl.pallas_call(
        functools.partial(sweep_kernel, depth),
        out_shape=sds(displacement.shape, F32),
        in_specs=[VMEM],
        out_specs=ANY,
        scratch_shapes=[
            pltpu.VMEM((3, tiles, depth + 16, LANES), F32),
            pltpu.VMEM((3, tiles, depth + 16, LANES), F32),
            pltpu.VMEM((3, tiles + 2, depth, LANES), F32),
            pltpu.VMEM((3, depth, cells), F32),
            dma((3,)),
        ],
        compiler_params=params(LIMIT),
        cost_estimate=pl.CostEstimate(flops=10**9, bytes_accessed=40 << 20, transcendentals=0),
        name="sweeps",
    )(u)

    return pl.pallas_call(
        functools.partial(seam_kernel, depth),
        out_shape=sds(displacement.shape, F32),
        in_specs=[VMEM, VMEM, VMEM, ANY],
        out_specs=ANY,
        scratch_shapes=[
            pltpu.VMEM((3, tiles, 40, LANES), F32),
            pltpu.VMEM((3, tiles, 40, LANES), F32),
            pltpu.VMEM((3, tiles + 2, 24, LANES), F32),
            pltpu.VMEM((2, 3, 8, cells), F32),
            dma((8,)),
        ],
        input_output_aliases={3: 0},
        compiler_params=params(LIMIT),
        name="seam_sweeps",
    )(u, u_even, u_odd, inside)


def solution(mesh):
    placed = (
        P("subj", None, "depth", None),
        P(),
        P(("grp", "subj"), None),
        P(("grp", "subj"), None, "depth", None),
        P(("grp", "subj"), None, "depth", None),
    )
    return jax.shard_map(
        local,
        mesh=mesh,
        in_specs=placed,
        out_specs=P(("grp", "subj"), None, "depth", None),
        check_vma=False,
    )
```

```python
import functools

import jax
import jax.numpy as jnp
from jax import lax
from jax.experimental import pallas as pl
from jax.experimental.pallas import tpu as pltpu
from jax.sharding import PartitionSpec as P

GY = 64
SWEEPS = 4
LANES = 128
RATE = 0.15
F32 = jnp.float32
BF16 = jnp.bfloat16
LIMIT = 48
LOAD = 46

ANY = pl.BlockSpec(memory_space=pl.ANY)
HBM = pl.BlockSpec(memory_space=pltpu.HBM)
VMEM = pl.BlockSpec(memory_space=pltpu.VMEM)


def params(mib):
    return pltpu.CompilerParams(vmem_limit_bytes=mib << 20)


def pair_swaps(count):
    def swaps(first):
        return [p for i in range(first, count - 1, 2) for p in ((i, i + 1), (i + 1, i))]

    return swaps(0), swaps(1)


def lateral_matrix(difference):
    row = lax.broadcasted_iota(jnp.int32, (2 * LANES, 2 * LANES), 0) & (LANES - 1)
    col = lax.broadcasted_iota(jnp.int32, (2 * LANES, 2 * LANES), 1)
    right = col >= LANES
    col = col & (LANES - 1)
    swap = jnp.where((row ^ col) == GY, 1.0, 0.0)
    same = (row & GY) == (col & GY)
    plus = jnp.where((row == col + 1) & same, 1.0, 0.0)
    minus = jnp.where((row == col - 1) & same, 1.0, 0.0)
    left = plus - minus if difference else plus + minus + swap
    return jnp.where(right, swap, left).astype(BF16)


def lateral(x, matrix):
    high = x.astype(BF16)
    low = (x - high.astype(F32)).astype(BF16)
    return jnp.dot(jnp.concatenate([high, low], 1), matrix, preferred_element_type=F32)


def low_half(rows):
    return lax.broadcasted_iota(jnp.int32, (rows, LANES), 1) < GY


def pieces_of(start, rows):
    done = start
    while done < start + rows:
        block = done // 16 * 16
        stop = min(block + 16, start + rows)
        yield block, done - block, stop - done
        done = stop


def force_stain(s_ref, k, mine, regions, own, recv, u_ref, r_ref, y_ref, matrix):
    tiles = s_ref.shape[1]
    parts = [s_ref[k, :, s0 : s0 + n, :] for s0, _, _, n in regions]
    x = parts[0] if len(parts) == 1 else jnp.concatenate(parts, 1)
    total = x.shape[1]
    p = lateral(x.reshape(tiles * total, LANES), matrix)
    y_ref[...] = p[:, :LANES].reshape(tiles, total, LANES)
    r_ref[1 : tiles + 1] = p[:, LANES:].reshape(tiles, total, LANES)
    base = 0
    for s0, f0, u0, n in regions:
        for block, skip, count in pieces_of(f0, n):
            z = block + skip - f0
            rows = slice(base + z, base + z + count)
            at = slice(u0 + z, u0 + z + count)
            s = s0 + z
            lo = low_half(count)
            r_now = r_ref[1, rows, :]
            before = jnp.where(lo, r_ref[0, rows, :], r_now)
            for c in range(tiles):
                r_next = r_ref[c + 2, rows, :]
                after = jnp.where(lo, r_now, r_next)
                gx = after - before
                before, r_now = after, r_next
                gy = y_ref[c, rows, :]
                gz = s_ref[k, c, s + 1 : s + 1 + count, :] - s_ref[k, c, s - 1 : s - 1 + count, :]
                place = (k, slice(block, block + 16), slice(c * LANES, (c + 1) * LANES))
                fixed = jnp.where(mine, own[place], recv[(0,) + place]).astype(F32)
                fixed = fixed[skip : skip + count]
                ux, uy, uz = u_ref[0, c, at, :], u_ref[1, c, at, :], u_ref[2, c, at, :]
                moved = (gx * ux + gy * uy) + gz * uz
                twice = (fixed - s_ref[k, c, s : s + count, :]) * 2.0 - moved
                denom = (gx * gx + gy * gy) + (gz * gz + (twice * twice + 2.0))
                w = twice * inverse(denom)
                u_ref[0, c, at, :] = ux + w * gx
                u_ref[1, c, at, :] = uy + w * gy
                u_ref[2, c, at, :] = uz + w * gz
        base += n


def inverse(x):
    r = pl.reciprocal(x, approx=True)
    return r * (2.0 - x * r)


def sweep(src, store, q, z0, rows, r_ref, matrix):
    tiles = src.shape[1]
    x = src[q, :, z0 : z0 + rows, :].reshape(tiles * rows, LANES)
    p = lateral(x, matrix)
    r_ref[q, 1 : tiles + 1] = p[:, LANES:].reshape(tiles, rows, LANES)
    inside = p[:, :LANES].reshape(tiles, rows, LANES)
    lo = low_half(rows)
    for c in range(tiles):
        depth = src[q, c, z0 - 1 : z0 - 1 + rows, :] + src[q, c, z0 + 1 : z0 + 1 + rows, :]
        across = jnp.where(lo, r_ref[q, c, :, :], r_ref[q, c + 2, :, :])
        store(c, src[q, c, z0 : z0 + rows, :] * (1.0 / RATE - 6.0) + depth + (inside[c] + across))


def clear_rim(ref, axis):
    shape = list(ref.shape)
    shape[axis] = 1
    at = [slice(None)] * len(shape)
    for i in (0, ref.shape[axis] - 1):
        at[axis] = slice(i, i + 1)
        ref[tuple(at)] = jnp.zeros(shape, F32)


def load_kernel(depth, subject, moved, s_ref, u_ref, even_send, odd_send, s_sem, u_sem):
    stains, tiles = s_ref.shape[:2]
    tall = depth // 8
    even = (lax.axis_index("depth") % 2) == 0

    def s_copy(t):
        return pltpu.make_async_copy(subject.at[:, t], s_ref.at[:, :, 8 + 8 * t : 16 + 8 * t, :], s_sem.at[t])

    def u_copy(t):
        return pltpu.make_async_copy(moved.at[:, t], u_ref.at[:, :, 8 + 8 * t : 16 + 8 * t, :], u_sem.at[t])

    order = (0, tall - 1) + tuple(range(1, tall - 1))
    for t in order:
        s_copy(t).start()
    for t in range(tall):
        u_copy(t).start()
    for t in order[:2]:
        s_copy(t).wait()
    for k in range(stains):
        for c in range(tiles):
            at = slice(c * LANES, (c + 1) * LANES)
            low, high = s_ref[k, c, 8:9, :], s_ref[k, c, depth + 7 : depth + 8, :]
            even_send[k : k + 1, at] = jnp.where(even, high, low)
            odd_send[k : k + 1, at] = jnp.where(even, low, high)
    for t in order[2:]:
        s_copy(t).wait()
    for t in range(tall):
        u_copy(t).wait()


def inner_kernel(depth, order_hbm, owner_hbm, s_ref, u_in, own, recv, u_ref, order, owner, r_ref, y_ref, o_sem):
    copies = [
        pltpu.make_async_copy(order_hbm, order, o_sem.at[0]),
        pltpu.make_async_copy(owner_hbm, owner, o_sem.at[1]),
    ]
    for copy in copies:
        copy.start()
    clear_rim(r_ref, 0)
    matrix = lateral_matrix(True)
    for copy in copies:
        copy.wait()
    for j in range(s_ref.shape[0]):
        k = order[0, j]
        mine = owner[k] == lax.axis_index("subj")
        force_stain(s_ref, k, mine, ((16, 8, 16, depth - 16),), own, recv, u_ref, r_ref, y_ref, matrix)


def edge_kernel(depth, order_hbm, owner_hbm, even_recv, odd_recv, own, recv, s_in, u_in, s_ref, u_ref, even_send,
                odd_send, order, owner, r_ref, y_ref, o_sem):
    stains, tiles = s_ref.shape[:2]
    copies = [
        pltpu.make_async_copy(order_hbm, order, o_sem.at[0]),
        pltpu.make_async_copy(owner_hbm, owner, o_sem.at[1]),
    ]
    for copy in copies:
        copy.start()
    even = (lax.axis_index("depth") % 2) == 0
    clear_rim(r_ref, 0)
    matrix = lateral_matrix(True)
    for c in range(tiles):
        at = slice(c * LANES, (c + 1) * LANES)
        a, b = even_recv[:, at], odd_recv[:, at]
        low, high = jnp.where(even, b, a), jnp.where(even, a, b)
        for k in range(stains):
            s_ref[k, c, 7:8, :] = low[k : k + 1]
            s_ref[k, c, depth + 8 : depth + 9, :] = high[k : k + 1]
    for copy in copies:
        copy.wait()
    for j in range(stains):
        k = order[0, j]
        mine = owner[k] == lax.axis_index("subj")
        regions = ((8, 0, 8, 8), (depth, depth - 8, depth, 8))
        force_stain(s_ref, k, mine, regions, own, recv, u_ref, r_ref, y_ref, matrix)
    n = SWEEPS
    for q in range(3):
        for c in range(tiles):
            at = slice(c * LANES, (c + 1) * LANES)
            low, high = u_ref[q, c, 8 : 8 + n, :], u_ref[q, c, 8 + depth - n : 8 + depth, :]
            even_send[q, :, at] = jnp.where(even, high, low)
            odd_send[q, :, at] = jnp.where(even, low, high)


def sweep_kernel(depth, u_ref, out, a_ref, b_ref, r_ref, o_ref, o_sem):
    clear_rim(r_ref, 1)
    matrix = lateral_matrix(False)
    src, dst = u_ref, a_ref
    for i in range(SWEEPS):
        final = i == SWEEPS - 1
        for q in range(3):

            def store(c, value, q=q, dst=dst, final=final):
                if final:
                    o_ref[q, :, c * LANES : (c + 1) * LANES] = value * RATE**SWEEPS
                else:
                    dst[q, c, 8 : 8 + depth, :] = value

            sweep(src, store, q, 8, depth, r_ref, matrix)
            if final:
                pltpu.make_async_copy(o_ref.at[q], out.at[0, q], o_sem.at[q]).start()
        src, dst = dst, (b_ref if dst is a_ref else a_ref)
    for q in range(3):
        pltpu.make_async_copy(o_ref.at[q], out.at[0, q], o_sem.at[q]).wait()


def seam_kernel(depth, u_ref, even_recv, odd_recv, before, out, a_ref, b_ref, r_ref, o_ref, sem):
    tiles = u_ref.shape[1]
    at_depth = lax.axis_index("depth")
    even = (at_depth % 2) == 0
    has_low = at_depth > 0
    has_high = at_depth < lax.axis_size("depth") - 1
    ends = (0, depth - 8)
    ins = [
        pltpu.make_async_copy(before.at[0, :, z : z + 8, :], o_ref.at[i], sem.at[i]) for i, z in enumerate(ends)
    ]
    outs = [
        pltpu.make_async_copy(o_ref.at[i, q], out.at[0, q, z : z + 8, :], sem.at[2 + 2 * q + i])
        for q in range(3)
        for i, z in enumerate(ends)
    ]
    for copy in ins:
        copy.start()
    clear_rim(r_ref, 1)
    n = SWEEPS
    for q in range(3):
        a_ref[q, :, 8:16, :] = u_ref[q, :, depth : depth + 8, :]
        a_ref[q, :, 24:32, :] = u_ref[q, :, 8:16, :]
        for c in range(tiles):
            at = slice(c * LANES, (c + 1) * LANES)
            x, y = even_recv[q, :, at], odd_recv[q, :, at]
            a_ref[q, c, 16 : 16 + n, :] = jnp.where(even, x, y)
            a_ref[q, c, 20 : 20 + n, :] = jnp.where(even, y, x)
    row = lax.broadcasted_iota(jnp.int32, (8, LANES), 0)
    keep = jnp.where(row < n, jnp.where(has_high, 1.0, 0.0), jnp.where(has_low, 1.0, 0.0))
    top = lax.broadcasted_iota(jnp.int32, (8, LANES), 0) < 4
    matrix = lateral_matrix(False)
    src, dst = a_ref, b_ref
    for i in range(SWEEPS):
        final = i == SWEEPS - 1
        if final:
            for copy in ins:
                copy.wait()
        for q in range(3):

            def store(c, value, q=q, dst=dst, final=final):
                at = slice(c * LANES, (c + 1) * LANES)
                if final:
                    value = value * RATE**SWEEPS
                    o_ref[0, q, :, at] = jnp.where(top, value[16:24], o_ref[0, q, :, at])
                    o_ref[1, q, :, at] = jnp.where(top, o_ref[1, q, :, at], value[0:8])
                else:
                    dst[q, c, 8:16, :] = value[0:8]
                    dst[q, c, 16:24, :] = value[8:16] * keep
                    dst[q, c, 24:32, :] = value[16:24]

            sweep(src, store, q, 8, 24, r_ref, matrix)
            if final:
                for copy in outs[2 * q : 2 * q + 2]:
                    copy.start()
        src, dst = dst, src
    for copy in outs:
        copy.wait()


def local(template, owner, order, subject, displacement):
    stains, depth, cells = subject.shape[1:]
    tiles = cells // LANES
    count = lax.axis_size("depth")
    even_pairs, odd_pairs = pair_swaps(count)

    recv = lax.ppermute(template, "subj", [(0, 1), (1, 0)])

    def tiled(a):
        return a.reshape(a.shape[1], depth // 8, 8, tiles, LANES).transpose(0, 1, 3, 2, 4)

    subject5, moved5 = tiled(subject), tiled(displacement)
    sds = jax.ShapeDtypeStruct
    dma = pltpu.SemaphoreType.DMA

    tall = depth // 8
    s_type = pltpu.VMEM((stains, tiles, depth + 16, LANES), F32)
    u_type = pltpu.VMEM((3, tiles, depth + 16, LANES), F32)
    send_type = pltpu.VMEM((3, SWEEPS, cells), F32)

    def force_scratch(planes):
        return [pltpu.VMEM((tiles + 2, planes, LANES), F32), pltpu.VMEM((tiles, planes, LANES), F32)]

    plane_type = pltpu.VMEM((stains, cells), F32)
    s, u, even_send, odd_send = pl.pallas_call(
        functools.partial(load_kernel, depth),
        out_shape=(s_type, u_type, plane_type, plane_type),
        in_specs=[HBM, HBM],
        out_specs=(VMEM,) * 4,
        scratch_shapes=[dma((tall,)), dma((tall,))],
        compiler_params=params(LOAD),
        name="load",
    )(subject5, moved5)

    even_recv = lax.ppermute(even_send, "depth", even_pairs)
    odd_recv = lax.ppermute(odd_send, "depth", odd_pairs)

    scalars = [pltpu.SMEM(order.shape, jnp.int32), pltpu.SMEM(owner.shape, jnp.int32)]
    own = template[0]
    u = pl.pallas_call(
        functools.partial(inner_kernel, depth),
        out_shape=u_type,
        in_specs=[HBM, HBM, VMEM, VMEM, VMEM, VMEM],
        out_specs=VMEM,
        scratch_shapes=scalars + force_scratch(depth - 16) + [dma((2,))],
        input_output_aliases={3: 0},
        compiler_params=params(20),
        cost_estimate=pl.CostEstimate(flops=4 * 10**8, bytes_accessed=10 << 20, transcendentals=0),
        name="inner_force",
    )(order, owner, s, u, own, recv)

    s, u, even_send, odd_send = pl.pallas_call(
        functools.partial(edge_kernel, depth),
        out_shape=(s_type, u_type, send_type, send_type),
        in_specs=[HBM, HBM] + [VMEM] * 6,
        out_specs=(VMEM, VMEM, VMEM, VMEM),
        scratch_shapes=scalars + force_scratch(16) + [dma((2,))],
        input_output_aliases={6: 0, 7: 1},
        compiler_params=params(20),
        cost_estimate=pl.CostEstimate(flops=10**8, bytes_accessed=8 << 20, transcendentals=0),
        name="edge_force",
    )(order, owner, even_recv, odd_recv, own, recv, s, u)

    u_even = lax.ppermute(even_send, "depth", even_pairs)
    u_odd = lax.ppermute(odd_send, "depth", odd_pairs)

    inside = pl.pallas_call(
        functools.partial(sweep_kernel, depth),
        out_shape=sds(displacement.shape, F32),
        in_specs=[VMEM],
        out_specs=ANY,
        scratch_shapes=[
            pltpu.VMEM((3, tiles, depth + 16, LANES), F32),
            pltpu.VMEM((3, tiles, depth + 16, LANES), F32),
            pltpu.VMEM((3, tiles + 2, depth, LANES), F32),
            pltpu.VMEM((3, depth, cells), F32),
            dma((3,)),
        ],
        compiler_params=params(LIMIT),
        cost_estimate=pl.CostEstimate(flops=10**9, bytes_accessed=40 << 20, transcendentals=0),
        name="sweeps",
    )(u)

    return pl.pallas_call(
        functools.partial(seam_kernel, depth),
        out_shape=sds(displacement.shape, F32),
        in_specs=[VMEM, VMEM, VMEM, ANY],
        out_specs=ANY,
        scratch_shapes=[
            pltpu.VMEM((3, tiles, 40, LANES), F32),
            pltpu.VMEM((3, tiles, 40, LANES), F32),
            pltpu.VMEM((3, tiles + 2, 24, LANES), F32),
            pltpu.VMEM((2, 3, 8, cells), F32),
            dma((8,)),
        ],
        input_output_aliases={3: 0},
        compiler_params=params(LIMIT),
        name="seam_sweeps",
    )(u, u_even, u_odd, inside)


def solution(mesh):
    placed = (
        P("subj", None, "depth", None),
        P(),
        P(("grp", "subj"), None),
        P(("grp", "subj"), None, "depth", None),
        P(("grp", "subj"), None, "depth", None),
    )
    return jax.shard_map(
        local,
        mesh=mesh,
        in_specs=placed,
        out_specs=P(("grp", "subj"), None, "depth", None),
        check_vma=False,
    )
```

```python
import functools

import jax
import jax.numpy as jnp
from jax import lax
from jax.experimental import pallas as pl
from jax.experimental.pallas import tpu as pltpu
from jax.sharding import PartitionSpec as P

GY = 64
SWEEPS = 4
LANES = 128
RATE = 0.15
F32 = jnp.float32
BF16 = jnp.bfloat16
LIMIT = 32
LOAD = 47

ANY = pl.BlockSpec(memory_space=pl.ANY)
HBM = pl.BlockSpec(memory_space=pltpu.HBM)
VMEM = pl.BlockSpec(memory_space=pltpu.VMEM)


def params(mib):
    return pltpu.CompilerParams(vmem_limit_bytes=mib << 20)


def pair_swaps(count):
    def swaps(first):
        return [p for i in range(first, count - 1, 2) for p in ((i, i + 1), (i + 1, i))]

    return swaps(0), swaps(1)


def lateral_matrix(difference):
    row = lax.broadcasted_iota(jnp.int32, (2 * LANES, 2 * LANES), 0) & (LANES - 1)
    col = lax.broadcasted_iota(jnp.int32, (2 * LANES, 2 * LANES), 1)
    right = col >= LANES
    col = col & (LANES - 1)
    swap = jnp.where((row ^ col) == GY, 1.0, 0.0)
    same = (row & GY) == (col & GY)
    plus = jnp.where((row == col + 1) & same, 1.0, 0.0)
    minus = jnp.where((row == col - 1) & same, 1.0, 0.0)
    left = plus - minus if difference else plus + minus + swap
    return jnp.where(right, swap, left).astype(BF16)


def lateral(x, matrix):
    high = x.astype(BF16)
    low = (x - high.astype(F32)).astype(BF16)
    return jnp.dot(jnp.concatenate([high, low], 1), matrix, preferred_element_type=F32)


def low_half(rows):
    return lax.broadcasted_iota(jnp.int32, (rows, LANES), 1) < GY


def pieces_of(start, rows):
    done = start
    while done < start + rows:
        block = done // 16 * 16
        stop = min(block + 16, start + rows)
        yield block, done - block, stop - done
        done = stop


def force_stain(s_ref, k, mine, regions, own, recv, moved, u_ref, r_ref, y_ref, matrix):
    tiles = s_ref.shape[1]
    parts = [s_ref[k, :, s0 : s0 + n, :] for s0, _, _, n in regions]
    x = parts[0] if len(parts) == 1 else jnp.concatenate(parts, 1)
    total = x.shape[1]
    p = lateral(x.reshape(tiles * total, LANES), matrix)
    y_ref[...] = p[:, :LANES].reshape(tiles, total, LANES)
    r_ref[1 : tiles + 1] = p[:, LANES:].reshape(tiles, total, LANES)
    base = 0
    for s0, f0, u0, n in regions:
        for block, skip, count in pieces_of(f0, n):
            z = block + skip - f0
            rows = slice(base + z, base + z + count)
            at = slice(u0 + z, u0 + z + count)
            s = s0 + z
            lo = low_half(count)
            r_now = r_ref[1, rows, :]
            before = jnp.where(lo, r_ref[0, rows, :], r_now)
            for c in range(tiles):
                r_next = r_ref[c + 2, rows, :]
                after = jnp.where(lo, r_now, r_next)
                gx = after - before
                before, r_now = after, r_next
                gy = y_ref[c, rows, :]
                gz = s_ref[k, c, s + 1 : s + 1 + count, :] - s_ref[k, c, s - 1 : s - 1 + count, :]
                place = (k, slice(block, block + 16), slice(c * LANES, (c + 1) * LANES))
                fixed = jnp.where(mine, own[place], recv[(0,) + place]).astype(F32)
                fixed = fixed[skip : skip + count]
                if moved is None:
                    ux, uy, uz = (u_ref[q, c, at, :] for q in range(3))
                else:
                    from_plane = slice(f0 + z, f0 + z + count)
                    ux, uy, uz = (moved[0, q, from_plane, c * LANES : (c + 1) * LANES] for q in range(3))
                slope = (gx * ux + gy * uy) + gz * uz
                twice = (fixed - s_ref[k, c, s : s + count, :]) * 2.0 - slope
                denom = (gx * gx + gy * gy) + (gz * gz + (twice * twice + 2.0))
                w = twice * inverse(denom)
                u_ref[0, c, at, :] = ux + w * gx
                u_ref[1, c, at, :] = uy + w * gy
                u_ref[2, c, at, :] = uz + w * gz
        base += n


def inverse(x):
    r = pl.reciprocal(x, approx=True)
    return r * (2.0 - x * r)


def sweep(src, store, q, z0, rows, r_ref, matrix):
    tiles = src.shape[1]
    x = src[q, :, z0 : z0 + rows, :].reshape(tiles * rows, LANES)
    p = lateral(x, matrix)
    r_ref[q, 1 : tiles + 1] = p[:, LANES:].reshape(tiles, rows, LANES)
    inside = p[:, :LANES].reshape(tiles, rows, LANES)
    lo = low_half(rows)
    for c in range(tiles):
        depth = src[q, c, z0 - 1 : z0 - 1 + rows, :] + src[q, c, z0 + 1 : z0 + 1 + rows, :]
        across = jnp.where(lo, r_ref[q, c, :, :], r_ref[q, c + 2, :, :])
        store(c, src[q, c, z0 : z0 + rows, :] * (1.0 / RATE - 6.0) + depth + (inside[c] + across))


def clear_rim(ref, axis):
    shape = list(ref.shape)
    shape[axis] = 1
    at = [slice(None)] * len(shape)
    for i in (0, ref.shape[axis] - 1):
        at[axis] = slice(i, i + 1)
        ref[tuple(at)] = jnp.zeros(shape, F32)


def load_kernel(depth, subject, s_ref, even_send, odd_send, s_sem):
    stains, tiles = s_ref.shape[:2]
    tall = depth // 8
    even = (lax.axis_index("depth") % 2) == 0

    def s_copy(t):
        return pltpu.make_async_copy(subject.at[:, t], s_ref.at[:, :, 8 + 8 * t : 16 + 8 * t, :], s_sem.at[t])

    order = (0, tall - 1) + tuple(range(1, tall - 1))
    for t in order:
        s_copy(t).start()
    for t in order[:2]:
        s_copy(t).wait()
    for k in range(stains):
        for c in range(tiles):
            at = slice(c * LANES, (c + 1) * LANES)
            low, high = s_ref[k, c, 8:9, :], s_ref[k, c, depth + 7 : depth + 8, :]
            even_send[k : k + 1, at] = jnp.where(even, high, low)
            odd_send[k : k + 1, at] = jnp.where(even, low, high)
    for t in order[2:]:
        s_copy(t).wait()


def inner_kernel(depth, order_hbm, owner_hbm, s_ref, moved, own, recv, u_ref, order, owner, r_ref, y_ref, o_sem):
    copies = [
        pltpu.make_async_copy(order_hbm, order, o_sem.at[0]),
        pltpu.make_async_copy(owner_hbm, owner, o_sem.at[1]),
    ]
    for copy in copies:
        copy.start()
    clear_rim(r_ref, 0)
    matrix = lateral_matrix(True)
    for copy in copies:
        copy.wait()
    for j in range(s_ref.shape[0]):
        k = order[0, j]
        mine = owner[k] == lax.axis_index("subj")
        force_stain(s_ref, k, mine, ((16, 8, 16, depth - 16),), own, recv, moved if j == 0 else None, u_ref, r_ref, y_ref, matrix)


def edge_kernel(depth, order_hbm, owner_hbm, even_recv, odd_recv, own, recv, moved, s_in, u_in, s_ref, u_ref, even_send,
                odd_send, order, owner, r_ref, y_ref, o_sem):
    stains, tiles = s_ref.shape[:2]
    copies = [
        pltpu.make_async_copy(order_hbm, order, o_sem.at[0]),
        pltpu.make_async_copy(owner_hbm, owner, o_sem.at[1]),
    ]
    for copy in copies:
        copy.start()
    even = (lax.axis_index("depth") % 2) == 0
    clear_rim(r_ref, 0)
    matrix = lateral_matrix(True)
    for c in range(tiles):
        at = slice(c * LANES, (c + 1) * LANES)
        a, b = even_recv[:, at], odd_recv[:, at]
        low, high = jnp.where(even, b, a), jnp.where(even, a, b)
        for k in range(stains):
            s_ref[k, c, 7:8, :] = low[k : k + 1]
            s_ref[k, c, depth + 8 : depth + 9, :] = high[k : k + 1]
    for copy in copies:
        copy.wait()
    for j in range(stains):
        k = order[0, j]
        mine = owner[k] == lax.axis_index("subj")
        regions = ((8, 0, 8, 8), (depth, depth - 8, depth, 8))
        force_stain(s_ref, k, mine, regions, own, recv, moved if j == 0 else None, u_ref, r_ref, y_ref, matrix)
    n = SWEEPS
    for q in range(3):
        for c in range(tiles):
            at = slice(c * LANES, (c + 1) * LANES)
            low, high = u_ref[q, c, 8 : 8 + n, :], u_ref[q, c, 8 + depth - n : 8 + depth, :]
            even_send[q, :, at] = jnp.where(even, high, low)
            odd_send[q, :, at] = jnp.where(even, low, high)


def sweep_kernel(depth, u_ref, o_ref, a_ref, b_ref, r_ref):
    clear_rim(r_ref, 1)
    matrix = lateral_matrix(False)
    src, dst = u_ref, a_ref
    for i in range(SWEEPS):
        final = i == SWEEPS - 1
        for q in range(3):

            def store(c, value, q=q, dst=dst, final=final):
                if final:
                    o_ref[q, :, c * LANES : (c + 1) * LANES] = value * RATE**SWEEPS
                else:
                    dst[q, c, 8 : 8 + depth, :] = value

            sweep(src, store, q, 8, depth, r_ref, matrix)
        src, dst = dst, (b_ref if dst is a_ref else a_ref)


def seam_kernel(depth, u_ref, even_recv, odd_recv, before, out, a_ref, b_ref, r_ref, o_ref, sem):
    tiles = u_ref.shape[1]
    at_depth = lax.axis_index("depth")
    even = (at_depth % 2) == 0
    has_low = at_depth > 0
    has_high = at_depth < lax.axis_size("depth") - 1
    ends = (0, depth - 8)
    inner = pl.ds(8, depth - 16)
    inside = [pltpu.make_async_copy(before.at[q, inner, :], out.at[0, q, inner, :], sem.at[6 + q]) for q in range(3)]
    outs = [
        pltpu.make_async_copy(o_ref.at[i, q], out.at[0, q, z : z + 8, :], sem.at[2 * q + i])
        for q in range(3)
        for i, z in enumerate(ends)
    ]
    for copy in inside:
        copy.start()
    clear_rim(r_ref, 1)
    n = SWEEPS
    for q in range(3):
        a_ref[q, :, 8:16, :] = u_ref[q, :, depth : depth + 8, :]
        a_ref[q, :, 24:32, :] = u_ref[q, :, 8:16, :]
        for c in range(tiles):
            at = slice(c * LANES, (c + 1) * LANES)
            x, y = even_recv[q, :, at], odd_recv[q, :, at]
            a_ref[q, c, 16 : 16 + n, :] = jnp.where(even, x, y)
            a_ref[q, c, 20 : 20 + n, :] = jnp.where(even, y, x)
    row = lax.broadcasted_iota(jnp.int32, (8, LANES), 0)
    keep = jnp.where(row < n, jnp.where(has_high, 1.0, 0.0), jnp.where(has_low, 1.0, 0.0))
    top = lax.broadcasted_iota(jnp.int32, (8, LANES), 0) < 4
    matrix = lateral_matrix(False)
    src, dst = a_ref, b_ref
    for i in range(SWEEPS):
        final = i == SWEEPS - 1
        for q in range(3):

            def store(c, value, q=q, dst=dst, final=final):
                at = slice(c * LANES, (c + 1) * LANES)
                if final:
                    value = value * RATE**SWEEPS
                    o_ref[0, q, :, at] = jnp.where(top, value[16:24], before[q, 0:8, at])
                    o_ref[1, q, :, at] = jnp.where(top, before[q, depth - 8 : depth, at], value[0:8])
                else:
                    dst[q, c, 8:16, :] = value[0:8]
                    dst[q, c, 16:24, :] = value[8:16] * keep
                    dst[q, c, 24:32, :] = value[16:24]

            sweep(src, store, q, 8, 24, r_ref, matrix)
            if final:
                for copy in outs[2 * q : 2 * q + 2]:
                    copy.start()
        src, dst = dst, src
    for copy in outs + inside:
        copy.wait()


def local(template, owner, order, subject, displacement):
    stains, depth, cells = subject.shape[1:]
    tiles = cells // LANES
    count = lax.axis_size("depth")
    even_pairs, odd_pairs = pair_swaps(count)

    recv = lax.ppermute(template, "subj", [(0, 1), (1, 0)])

    def tiled(a):
        return a.reshape(a.shape[1], depth // 8, 8, tiles, LANES).transpose(0, 1, 3, 2, 4)

    subject5 = tiled(subject)
    sds = jax.ShapeDtypeStruct
    dma = pltpu.SemaphoreType.DMA

    tall = depth // 8
    s_type = pltpu.VMEM((stains, tiles, depth + 16, LANES), F32)
    u_type = pltpu.VMEM((3, tiles, depth + 16, LANES), F32)
    send_type = pltpu.VMEM((3, SWEEPS, cells), F32)

    def force_scratch(planes):
        return [pltpu.VMEM((tiles + 2, planes, LANES), F32), pltpu.VMEM((tiles, planes, LANES), F32)]

    plane_type = pltpu.VMEM((stains, cells), F32)
    s, even_send, odd_send = pl.pallas_call(
        functools.partial(load_kernel, depth),
        out_shape=(s_type, plane_type, plane_type),
        in_specs=[HBM],
        out_specs=(VMEM,) * 3,
        scratch_shapes=[dma((tall,))],
        compiler_params=params(LOAD),
        cost_estimate=pl.CostEstimate(flops=4 * 10**9, bytes_accessed=24 << 20, transcendentals=0),
        name="load",
    )(subject5)

    even_recv = lax.ppermute(even_send, "depth", even_pairs)
    odd_recv = lax.ppermute(odd_send, "depth", odd_pairs)

    scalars = [pltpu.SMEM(order.shape, jnp.int32), pltpu.SMEM(owner.shape, jnp.int32)]
    own = template[0]
    u = pl.pallas_call(
        functools.partial(inner_kernel, depth),
        out_shape=u_type,
        in_specs=[HBM, HBM, VMEM, VMEM, VMEM, VMEM],
        out_specs=VMEM,
        scratch_shapes=scalars + force_scratch(depth - 16) + [dma((2,))],
        compiler_params=params(20),
        cost_estimate=pl.CostEstimate(flops=4 * 10**8, bytes_accessed=10 << 20, transcendentals=0),
        name="inner_force",
    )(order, owner, s, displacement, own, recv)

    s, u, even_send, odd_send = pl.pallas_call(
        functools.partial(edge_kernel, depth),
        out_shape=(s_type, u_type, send_type, send_type),
        in_specs=[HBM, HBM] + [VMEM] * 7,
        out_specs=(VMEM, VMEM, VMEM, VMEM),
        scratch_shapes=scalars + force_scratch(16) + [dma((2,))],
        input_output_aliases={7: 0, 8: 1},
        compiler_params=params(20),
        cost_estimate=pl.CostEstimate(flops=10**8, bytes_accessed=8 << 20, transcendentals=0),
        name="edge_force",
    )(order, owner, even_recv, odd_recv, own, recv, displacement, s, u)

    u_even = lax.ppermute(even_send, "depth", even_pairs)
    u_odd = lax.ppermute(odd_send, "depth", odd_pairs)

    inside = pl.pallas_call(
        functools.partial(sweep_kernel, depth),
        out_shape=pltpu.VMEM((3, depth, cells), F32),
        in_specs=[VMEM],
        out_specs=VMEM,
        scratch_shapes=[
            pltpu.VMEM((3, tiles, depth + 16, LANES), F32),
            pltpu.VMEM((3, tiles, depth + 16, LANES), F32),
            pltpu.VMEM((3, tiles + 2, depth, LANES), F32),
        ],
        compiler_params=params(LIMIT),
        cost_estimate=pl.CostEstimate(flops=10**9, bytes_accessed=40 << 20, transcendentals=0),
        name="sweeps",
    )(u)

    return pl.pallas_call(
        functools.partial(seam_kernel, depth),
        out_shape=sds(displacement.shape, F32),
        in_specs=[VMEM, VMEM, VMEM, VMEM],
        out_specs=ANY,
        scratch_shapes=[
            pltpu.VMEM((3, tiles, 40, LANES), F32),
            pltpu.VMEM((3, tiles, 40, LANES), F32),
            pltpu.VMEM((3, tiles + 2, 24, LANES), F32),
            pltpu.VMEM((2, 3, 8, cells), F32),
            dma((9,)),
        ],
        compiler_params=params(LIMIT),
        name="seam_sweeps",
    )(u, u_even, u_odd, inside)


def solution(mesh):
    placed = (
        P("subj", None, "depth", None),
        P(),
        P(("grp", "subj"), None),
        P(("grp", "subj"), None, "depth", None),
        P(("grp", "subj"), None, "depth", None),
    )
    return jax.shard_map(
        local,
        mesh=mesh,
        in_specs=placed,
        out_specs=P(("grp", "subj"), None, "depth", None),
        check_vma=False,
    )
```

```python
import functools

import jax
import jax.numpy as jnp
from jax import lax
from jax.experimental import pallas as pl
from jax.experimental.pallas import tpu as pltpu
from jax.sharding import PartitionSpec as P

GY = 64
SWEEPS = 4
LANES = 128
RATE = 0.15
F32 = jnp.float32
BF16 = jnp.bfloat16
LIMIT = 32
LOAD = 47

ANY = pl.BlockSpec(memory_space=pl.ANY)
HBM = pl.BlockSpec(memory_space=pltpu.HBM)
VMEM = pl.BlockSpec(memory_space=pltpu.VMEM)


def params(mib):
    return pltpu.CompilerParams(vmem_limit_bytes=mib << 20)


def pair_swaps(count):
    def swaps(first):
        return [p for i in range(first, count - 1, 2) for p in ((i, i + 1), (i + 1, i))]

    return swaps(0), swaps(1)


def lateral_matrix(difference):
    row = lax.broadcasted_iota(jnp.int32, (2 * LANES, 2 * LANES), 0) & (LANES - 1)
    col = lax.broadcasted_iota(jnp.int32, (2 * LANES, 2 * LANES), 1)
    right = col >= LANES
    col = col & (LANES - 1)
    swap = jnp.where((row ^ col) == GY, 1.0, 0.0)
    same = (row & GY) == (col & GY)
    plus = jnp.where((row == col + 1) & same, 1.0, 0.0)
    minus = jnp.where((row == col - 1) & same, 1.0, 0.0)
    left = plus - minus if difference else plus + minus + swap
    return jnp.where(right, swap, left).astype(BF16)


def lateral(x, matrix):
    high = x.astype(BF16)
    low = (x - high.astype(F32)).astype(BF16)
    return jnp.dot(jnp.concatenate([high, low], 1), matrix, preferred_element_type=F32)


def low_half(rows):
    return lax.broadcasted_iota(jnp.int32, (rows, LANES), 1) < GY


def pieces_of(start, rows):
    done = start
    while done < start + rows:
        block = done // 16 * 16
        stop = min(block + 16, start + rows)
        yield block, done - block, stop - done
        done = stop


def force_stain(s_ref, k, mine, regions, own, recv, moved, u_ref, r_ref, y_ref, matrix):
    tiles = s_ref.shape[1]
    parts = [s_ref[k, :, s0 : s0 + n, :] for s0, _, _, n in regions]
    x = parts[0] if len(parts) == 1 else jnp.concatenate(parts, 1)
    total = x.shape[1]
    p = lateral(x.reshape(tiles * total, LANES), matrix)
    y_ref[...] = p[:, :LANES].reshape(tiles, total, LANES)
    r_ref[1 : tiles + 1] = p[:, LANES:].reshape(tiles, total, LANES)
    base = 0
    for s0, f0, u0, n in regions:
        for block, skip, count in pieces_of(f0, n):
            z = block + skip - f0
            rows = slice(base + z, base + z + count)
            at = slice(u0 + z, u0 + z + count)
            s = s0 + z
            lo = low_half(count)
            r_now = r_ref[1, rows, :]
            before = jnp.where(lo, r_ref[0, rows, :], r_now)
            for c in range(tiles):
                r_next = r_ref[c + 2, rows, :]
                after = jnp.where(lo, r_now, r_next)
                gx = after - before
                before, r_now = after, r_next
                gy = y_ref[c, rows, :]
                gz = s_ref[k, c, s + 1 : s + 1 + count, :] - s_ref[k, c, s - 1 : s - 1 + count, :]
                place = (k, slice(block, block + 16), slice(c * LANES, (c + 1) * LANES))
                fixed = jnp.where(mine, own[place], recv[(0,) + place]).astype(F32)
                fixed = fixed[skip : skip + count]
                if moved is None:
                    ux, uy, uz = (u_ref[q, c, at, :] for q in range(3))
                else:
                    from_plane = slice(f0 + z, f0 + z + count)
                    ux, uy, uz = (moved[0, q, from_plane, c * LANES : (c + 1) * LANES] for q in range(3))
                slope = (gx * ux + gy * uy) + gz * uz
                twice = (fixed - s_ref[k, c, s : s + count, :]) * 2.0 - slope
                denom = (gx * gx + gy * gy) + (gz * gz + (twice * twice + 2.0))
                w = twice * inverse(denom)
                u_ref[0, c, at, :] = ux + w * gx
                u_ref[1, c, at, :] = uy + w * gy
                u_ref[2, c, at, :] = uz + w * gz
        base += n


def inverse(x):
    r = pl.reciprocal(x, approx=True)
    return r * (2.0 - x * r)


def sweep(src, store, q, z0, rows, r_ref, matrix):
    tiles = src.shape[1]
    x = src[q, :, z0 : z0 + rows, :].reshape(tiles * rows, LANES)
    p = lateral(x, matrix)
    r_ref[q, 1 : tiles + 1] = p[:, LANES:].reshape(tiles, rows, LANES)
    inside = p[:, :LANES].reshape(tiles, rows, LANES)
    lo = low_half(rows)
    for c in range(tiles):
        depth = src[q, c, z0 - 1 : z0 - 1 + rows, :] + src[q, c, z0 + 1 : z0 + 1 + rows, :]
        across = jnp.where(lo, r_ref[q, c, :, :], r_ref[q, c + 2, :, :])
        store(c, src[q, c, z0 : z0 + rows, :] * (1.0 / RATE - 6.0) + depth + (inside[c] + across))


def clear_rim(ref, axis):
    shape = list(ref.shape)
    shape[axis] = 1
    at = [slice(None)] * len(shape)
    for i in (0, ref.shape[axis] - 1):
        at[axis] = slice(i, i + 1)
        ref[tuple(at)] = jnp.zeros(shape, F32)


def load_kernel(depth, subject, s_ref, even_send, odd_send, s_sem):
    stains, tiles = s_ref.shape[:2]
    tall = depth // 8
    even = (lax.axis_index("depth") % 2) == 0

    def s_copy(t):
        return pltpu.make_async_copy(subject.at[:, t], s_ref.at[:, :, 8 + 8 * t : 16 + 8 * t, :], s_sem.at[t])

    order = (0, tall - 1) + tuple(range(1, tall - 1))
    for t in order:
        s_copy(t).start()
    for t in order[:2]:
        s_copy(t).wait()
    for k in range(stains):
        for c in range(tiles):
            at = slice(c * LANES, (c + 1) * LANES)
            low, high = s_ref[k, c, 8:9, :], s_ref[k, c, depth + 7 : depth + 8, :]
            even_send[k : k + 1, at] = jnp.where(even, high, low)
            odd_send[k : k + 1, at] = jnp.where(even, low, high)
    for t in order[2:]:
        s_copy(t).wait()


def inner_kernel(depth, order_hbm, owner_hbm, s_ref, moved, own, recv, u_ref, order, owner, r_ref, y_ref, o_sem):
    copies = [
        pltpu.make_async_copy(order_hbm, order, o_sem.at[0]),
        pltpu.make_async_copy(owner_hbm, owner, o_sem.at[1]),
    ]
    for copy in copies:
        copy.start()
    clear_rim(r_ref, 0)
    matrix = lateral_matrix(True)
    for copy in copies:
        copy.wait()
    for j in range(s_ref.shape[0]):
        k = order[0, j]
        mine = owner[k] == lax.axis_index("subj")
        force_stain(s_ref, k, mine, ((16, 8, 16, depth - 16),), own, recv, moved if j == 0 else None, u_ref, r_ref, y_ref, matrix)


def edge_kernel(depth, order_hbm, owner_hbm, even_recv, odd_recv, own, recv, moved, s_in, u_in, s_ref, u_ref, even_send,
                odd_send, order, owner, r_ref, y_ref, o_sem, t_ref):
    stains, tiles = s_ref.shape[:2]
    copies = [
        pltpu.make_async_copy(order_hbm, order, o_sem.at[0]),
        pltpu.make_async_copy(owner_hbm, owner, o_sem.at[1]),
    ]
    for copy in copies:
        copy.start()
    even = (lax.axis_index("depth") % 2) == 0
    clear_rim(r_ref, 0)
    t_ref[...] = jnp.zeros(t_ref.shape, F32)
    matrix = lateral_matrix(True)
    for c in range(tiles):
        at = slice(c * LANES, (c + 1) * LANES)
        a, b = even_recv[:, at], odd_recv[:, at]
        low, high = jnp.where(even, b, a), jnp.where(even, a, b)
        for k in range(stains):
            s_ref[k, c, 7:8, :] = low[k : k + 1]
            s_ref[k, c, depth + 8 : depth + 9, :] = high[k : k + 1]
    for copy in copies:
        copy.wait()
    for j in range(stains):
        k = order[0, j]
        mine = owner[k] == lax.axis_index("subj")
        regions = ((8, 0, 8, 8), (depth, depth - 8, depth, 8))
        force_stain(s_ref, k, mine, regions, own, recv, moved if j == 0 else None, u_ref, r_ref, y_ref, matrix)
    n = SWEEPS
    for send, up in ((even_send, even), (odd_send, jnp.logical_not(even))):
        for c in range(tiles):
            at = slice(c * LANES, (c + 1) * LANES)
            for q in range(3):
                low, high = u_ref[q, c, 8 : 8 + n, :], u_ref[q, c, 8 + depth - n : 8 + depth, :]
                t_ref[n * q : n * q + n, at] = jnp.where(up, high, low)
                near = jnp.where(up, u_ref[q, c, 7 + depth : 8 + depth, :], u_ref[q, c, 8:9, :])
                t_ref[3 * n + q : 3 * n + q + 1, at] = near - near.astype(BF16).astype(F32)
            send[:, at] = t_ref[:, at].astype(BF16)


def sweep_kernel(depth, u_ref, o_ref, a_ref, b_ref, r_ref):
    clear_rim(r_ref, 1)
    matrix = lateral_matrix(False)
    src, dst = u_ref, a_ref
    for i in range(SWEEPS):
        final = i == SWEEPS - 1
        for q in range(3):

            def store(c, value, q=q, dst=dst, final=final):
                if final:
                    o_ref[q, :, c * LANES : (c + 1) * LANES] = value * RATE**SWEEPS
                else:
                    dst[q, c, 8 : 8 + depth, :] = value

            sweep(src, store, q, 8, depth, r_ref, matrix)
        src, dst = dst, (b_ref if dst is a_ref else a_ref)


def seam_kernel(depth, u_ref, even_recv, odd_recv, before, out, a_ref, b_ref, r_ref, o_ref, sem, h_ref):
    tiles = u_ref.shape[1]
    at_depth = lax.axis_index("depth")
    even = (at_depth % 2) == 0
    has_low = at_depth > 0
    has_high = at_depth < lax.axis_size("depth") - 1
    ends = (0, depth - 8)
    inner = pl.ds(8, depth - 16)
    inside = [pltpu.make_async_copy(before.at[q, inner, :], out.at[0, q, inner, :], sem.at[6 + q]) for q in range(3)]
    outs = [
        pltpu.make_async_copy(o_ref.at[i, q], out.at[0, q, z : z + 8, :], sem.at[2 * q + i])
        for q in range(3)
        for i, z in enumerate(ends)
    ]
    for copy in inside:
        copy.start()
    clear_rim(r_ref, 1)
    n = SWEEPS
    for q in range(3):
        a_ref[q, :, 8:16, :] = u_ref[q, :, depth : depth + 8, :]
        a_ref[q, :, 24:32, :] = u_ref[q, :, 8:16, :]
    for c in range(tiles):
        at = slice(c * LANES, (c + 1) * LANES)
        x, y = even_recv[:, at].astype(F32), odd_recv[:, at].astype(F32)
        h_ref[0, :, at] = jnp.where(even, x, y)
        h_ref[1, :, at] = jnp.where(even, y, x)
        for q in range(3):
            rest = slice(3 * n + q, 3 * n + q + 1)
            a_ref[q, c, 16 : 16 + n, :] = h_ref[0, n * q : n * q + n, at]
            a_ref[q, c, 20 : 20 + n, :] = h_ref[1, n * q : n * q + n, at]
            a_ref[q, c, 16:17, :] = h_ref[0, n * q : n * q + 1, at] + h_ref[0, rest, at]
            a_ref[q, c, 23:24, :] = h_ref[1, n * q + n - 1 : n * q + n, at] + h_ref[1, rest, at]
    row = lax.broadcasted_iota(jnp.int32, (8, LANES), 0)
    keep = jnp.where(row < n, jnp.where(has_high, 1.0, 0.0), jnp.where(has_low, 1.0, 0.0))
    top = lax.broadcasted_iota(jnp.int32, (8, LANES), 0) < 4
    matrix = lateral_matrix(False)
    src, dst = a_ref, b_ref
    for i in range(SWEEPS):
        final = i == SWEEPS - 1
        for q in range(3):

            def store(c, value, q=q, dst=dst, final=final):
                at = slice(c * LANES, (c + 1) * LANES)
                if final:
                    value = value * RATE**SWEEPS
                    o_ref[0, q, :, at] = jnp.where(top, value[16:24], before[q, 0:8, at])
                    o_ref[1, q, :, at] = jnp.where(top, before[q, depth - 8 : depth, at], value[0:8])
                else:
                    dst[q, c, 8:16, :] = value[0:8]
                    dst[q, c, 16:24, :] = value[8:16] * keep
                    dst[q, c, 24:32, :] = value[16:24]

            sweep(src, store, q, 8, 24, r_ref, matrix)
            if final:
                for copy in outs[2 * q : 2 * q + 2]:
                    copy.start()
        src, dst = dst, src
    for copy in outs + inside:
        copy.wait()


def local(template, owner, order, subject, displacement):
    stains, depth, cells = subject.shape[1:]
    tiles = cells // LANES
    count = lax.axis_size("depth")
    even_pairs, odd_pairs = pair_swaps(count)

    recv = lax.ppermute(template, "subj", [(0, 1), (1, 0)])

    def tiled(a):
        return a.reshape(a.shape[1], depth // 8, 8, tiles, LANES).transpose(0, 1, 3, 2, 4)

    subject5 = tiled(subject)
    sds = jax.ShapeDtypeStruct
    dma = pltpu.SemaphoreType.DMA

    tall = depth // 8
    s_type = pltpu.VMEM((stains, tiles, depth + 16, LANES), F32)
    u_type = pltpu.VMEM((3, tiles, depth + 16, LANES), F32)
    send_type = pltpu.VMEM((16, cells), BF16)

    def force_scratch(planes):
        return [pltpu.VMEM((tiles + 2, planes, LANES), F32), pltpu.VMEM((tiles, planes, LANES), F32)]

    plane_type = pltpu.VMEM((stains, cells), F32)
    s, even_send, odd_send = pl.pallas_call(
        functools.partial(load_kernel, depth),
        out_shape=(s_type, plane_type, plane_type),
        in_specs=[HBM],
        out_specs=(VMEM,) * 3,
        scratch_shapes=[dma((tall,))],
        compiler_params=params(LOAD),
        cost_estimate=pl.CostEstimate(flops=4 * 10**9, bytes_accessed=24 << 20, transcendentals=0),
        name="load",
    )(subject5)

    even_recv = lax.ppermute(even_send, "depth", even_pairs)
    odd_recv = lax.ppermute(odd_send, "depth", odd_pairs)

    scalars = [pltpu.SMEM(order.shape, jnp.int32), pltpu.SMEM(owner.shape, jnp.int32)]
    own = template[0]
    u = pl.pallas_call(
        functools.partial(inner_kernel, depth),
        out_shape=u_type,
        in_specs=[HBM, HBM, VMEM, VMEM, VMEM, VMEM],
        out_specs=VMEM,
        scratch_shapes=scalars + force_scratch(depth - 16) + [dma((2,))],
        compiler_params=params(20),
        cost_estimate=pl.CostEstimate(flops=4 * 10**8, bytes_accessed=10 << 20, transcendentals=0),
        name="inner_force",
    )(order, owner, s, displacement, own, recv)

    s, u, even_send, odd_send = pl.pallas_call(
        functools.partial(edge_kernel, depth),
        out_shape=(s_type, u_type, send_type, send_type),
        in_specs=[HBM, HBM] + [VMEM] * 7,
        out_specs=(VMEM, VMEM, VMEM, VMEM),
        scratch_shapes=scalars + force_scratch(16) + [dma((2,)), pltpu.VMEM((16, cells), F32)],
        input_output_aliases={7: 0, 8: 1},
        compiler_params=params(20),
        cost_estimate=pl.CostEstimate(flops=10**8, bytes_accessed=8 << 20, transcendentals=0),
        name="edge_force",
    )(order, owner, even_recv, odd_recv, own, recv, displacement, s, u)

    u_even = lax.ppermute(even_send, "depth", even_pairs)
    u_odd = lax.ppermute(odd_send, "depth", odd_pairs)

    inside = pl.pallas_call(
        functools.partial(sweep_kernel, depth),
        out_shape=pltpu.VMEM((3, depth, cells), F32),
        in_specs=[VMEM],
        out_specs=VMEM,
        scratch_shapes=[
            pltpu.VMEM((3, tiles, depth + 16, LANES), F32),
            pltpu.VMEM((3, tiles, depth + 16, LANES), F32),
            pltpu.VMEM((3, tiles + 2, depth, LANES), F32),
        ],
        compiler_params=params(LIMIT),
        cost_estimate=pl.CostEstimate(flops=10**9, bytes_accessed=40 << 20, transcendentals=0),
        name="sweeps",
    )(u)

    return pl.pallas_call(
        functools.partial(seam_kernel, depth),
        out_shape=sds(displacement.shape, F32),
        in_specs=[VMEM, VMEM, VMEM, VMEM],
        out_specs=ANY,
        scratch_shapes=[
            pltpu.VMEM((3, tiles, 40, LANES), F32),
            pltpu.VMEM((3, tiles, 40, LANES), F32),
            pltpu.VMEM((3, tiles + 2, 24, LANES), F32),
            pltpu.VMEM((2, 3, 8, cells), F32),
            dma((9,)),
            pltpu.VMEM((2, 16, cells), F32),
        ],
        compiler_params=params(LIMIT),
        name="seam_sweeps",
    )(u, u_even, u_odd, inside)


def solution(mesh):
    placed = (
        P("subj", None, "depth", None),
        P(),
        P(("grp", "subj"), None),
        P(("grp", "subj"), None, "depth", None),
        P(("grp", "subj"), None, "depth", None),
    )
    return jax.shard_map(
        local,
        mesh=mesh,
        in_specs=placed,
        out_specs=P(("grp", "subj"), None, "depth", None),
        check_vma=False,
    )
```
